128 devices in a mesh: box: 128 (over x, y, z, core).
Axes of the slice: x: 4, y: 4, z: 4, core: 2. Of those that a mesh axis runs over, the one named last changes fastest.
Arguments:
- multipoles: bfloat16 [48, 49152], P(None, 'box'), may hold values from -6 to 6
- partners: int32 [189, 49152], P(None, 'box'), may hold values from 0 to 191, as said below
- partner_offset: int32 [189, 49152], P(None, 'box'), may hold values from 0 to 29, as said below
- classes: int32 [189, 49152], P(None, 'box'), may hold values from 0 to 315, as said below
- m2l_ops: bfloat16 [48, 15168], replicated, may hold values from -0.0625 to 0.0625
- m2m_ops: bfloat16 [48, 384], replicated, may hold values from -0.3125 to 0.3125
- coarse_ops: float32 [48, 48], replicated, may hold values from -0.875 to 0.875
- coupling: float32 [64, 64], replicated, may hold values from -0.75 to 0.75
- l2l_ops: float32 [48, 384], replicated, may hold values from -0.875 to 0.875
Outputs:
- locals_out: float32 [48, 49152], P(None, 'box')
- parents: float32 [48, 6144], P(None, 'box')
The draws below stay inside these ranges and needn't reach their ends.
Inputs may be any that keep to these rules, and one draw needn't show every extreme that they name: `partners`: the source box s lies on the same device as the box, or among the first 48 or last 48 boxes of a device at most 7 devices away; every device has a source exactly 7 devices away. `partner_offset`: together with partners it names a box of the grid. classes[k, b] depends only on b mod 8 and k, and the 189 classes of one box are all different.
All inputs are finite; a program needn't handle non-finite values.
Results may differ from the reference program's by a relative error of at most 0.00035.
Values may be sent and summed in bfloat16 or wider, within the bound.
A program may use at most 128 MiB of HBM per device.

```python
import jax
import jax.numpy as jnp
from jax import lax

R = 48
K = 189
CLASSES = 316
REACH = 7
COARSE = 64
BOX_DEV = 384
RIM = 48
BOXES = 49152


def global_sources(key):
    keys = jax.random.split(key, 6)
    device_count = BOXES // BOX_DEV
    boxes = jnp.arange(BOXES, dtype=jnp.int32)
    device = boxes // BOX_DEV
    thresholds = jax.random.randint(keys[0], (device_count,), 2, 9)
    rolls = jax.random.randint(keys[1], (K, BOXES), 0, 16)
    slot_row = jnp.arange(K, dtype=jnp.int32)[:, None]
    forced = jnp.logical_and(boxes[None, :] % BOX_DEV == 0, slot_row == 0)
    remote = jnp.logical_or(rolls < thresholds[device][None, :], forced)
    local_pick = device[None, :] * BOX_DEV + jax.random.randint(keys[2], (K, BOXES), 0, BOX_DEV)
    magnitude = jax.random.randint(keys[3], (K, BOXES), 1, REACH + 1)
    magnitude = jnp.where(forced, REACH, magnitude)
    direction = jax.random.randint(keys[4], (K, BOXES), 0, 2) * 2 - 1
    target = device[None, :] + direction * magnitude
    outside = jnp.logical_or(target < 0, target >= device_count)
    target = jnp.where(outside, device[None, :] - direction * magnitude, target)
    rim_pick = jax.random.randint(keys[5], (K, BOXES), 0, 2 * RIM)
    within = jnp.where(rim_pick < RIM, rim_pick, BOX_DEV - 2 * RIM + rim_pick)
    remote_pick = target * BOX_DEV + within
    return (jnp.where(remote, remote_pick, local_pick).astype(jnp.int32), device)


def draw_partners(key, part):
    sources, device = global_sources(key)
    return (sources % (BOX_DEV // 2)).astype(jnp.int32)


def draw_partner_offset(key, part):
    sources, device = global_sources(key)
    halves = sources // (BOX_DEV // 2)
    return (halves - 2 * device[None, :] + 2 * REACH).astype(jnp.int32)


def draw_classes(key, part):
    key = jax.random.fold_in(key, 23)
    keys = jax.random.split(key, 2)
    starts = jax.random.randint(keys[0], (8,), 0, CLASSES)
    strides = jax.random.randint(keys[1], (8,), 0, 39) * 2 + 1
    octant = jnp.arange(BOXES, dtype=jnp.int32) % 8
    slot_row = jnp.arange(K, dtype=jnp.int32)[:, None]
    values = (starts[octant][None, :] + slot_row * strides[octant][None, :]) % CLASSES
    return values.astype(jnp.int32)


def level_of(rng, shape, cuts, smallest, largest):
    level, own = 1.0, jax.random.fold_in(rng, 6)
    for dim, shards_of in cuts:
        steps = jnp.exp(jax.random.uniform(jax.random.fold_in(own, dim), (shards_of,), jnp.float32, smallest / len(cuts), largest / len(cuts)))
        level = level * jnp.repeat(steps, shape[dim] // shards_of).reshape([-1 if axis == dim else 1 for axis in range(len(shape))])
    return level


def noise(rng, shape, deviation, bound, cuts=(), kind=jnp.bfloat16):
    result = deviation * jax.random.normal(rng, shape, jnp.float32)
    if cuts:
        result = result * level_of(rng, shape, cuts, -0.22, 0.18)
    return jnp.clip(result, -bound, bound).astype(kind)


def setup_inputs(seed: int = 0) -> dict:
    splits = jax.random.split(jax.random.key(seed), 10)
    multipoles = noise(splits[0], (R, BOXES), 1.0, 6.0, ((1, 128),))
    partners = draw_partners(jax.random.fold_in(splits[9], 71), 0)
    partner_offset = draw_partner_offset(jax.random.fold_in(splits[9], 71), 0)
    classes = draw_classes(jax.random.fold_in(splits[9], 71), 0)
    m2l_ops = noise(splits[4], (R, CLASSES * R), (R * K) ** -0.5, 0.0625)
    m2m_ops = noise(splits[5], (R, 8 * R), (8 * R) ** -0.5, 0.3125)
    coarse_ops = noise(splits[6], (R, R), R ** -0.5, 0.875, (), jnp.float32)
    coupling = noise(splits[7], (COARSE, COARSE), COARSE ** -0.5, 0.75, (), jnp.float32)
    l2l_ops = noise(splits[8], (R, 8 * R), R ** -0.5, 0.875, (), jnp.float32)
    return {"multipoles": multipoles, "partners": partners, "partner_offset": partner_offset, "classes": classes, "m2l_ops": m2l_ops, "m2m_ops": m2m_ops, "coarse_ops": coarse_ops, "coupling": coupling, "l2l_ops": l2l_ops}


def octant_terms(table, chosen, classes_row, cube):
    rank = table.shape[0]
    slots = chosen.shape[0]
    gathered = jnp.take(table, chosen, axis=1)
    stacked = gathered.reshape(rank * slots, chosen.shape[1])
    picked = jnp.take(cube, classes_row, axis=1)
    operator = jnp.transpose(picked, (0, 2, 1)).reshape(rank, rank * slots)
    return jnp.dot(operator, stacked, preferred_element_type=jnp.float32)


def reference(multipoles, partners, partner_offset, classes, m2l_ops, m2m_ops, coarse_ops, coupling, l2l_ops):
    rank, total = multipoles.shape
    cube = m2l_ops.reshape(rank, CLASSES, rank)
    width = BOX_DEV // 8
    blocks = total // 8 // width
    group = total // (8 * COARSE)
    highest = lax.Precision.HIGHEST
    half_size = BOX_DEV // 2
    owners = (jnp.arange(total, dtype=jnp.int32) // BOX_DEV).astype(jnp.int32)
    children = jnp.transpose(multipoles.reshape(rank, total // 8, 8), (2, 0, 1)).reshape(8 * rank, total // 8)
    parents = jnp.dot(m2m_ops, children, preferred_element_type=jnp.float32)
    coarse = jnp.sum(parents.reshape(rank, COARSE, group), axis=2) * jnp.float32(group ** -0.5)
    far = jnp.dot(jnp.dot(coarse_ops, coarse, precision=highest), coupling.T, precision=highest)
    outputs = []
    for octant in range(8):
        own_dev = owners[octant::8][None, :]
        chosen = ((2 * own_dev - 2 * REACH + partner_offset[:, octant::8]) * half_size + partners[:, octant::8]).astype(jnp.int32)
        tiles = jnp.transpose(chosen.reshape(K, blocks, width), (1, 0, 2))
        classes_row = classes[:, octant]
        near = lax.map(lambda tile: octant_terms(multipoles, tile, classes_row, cube), tiles)
        near = jnp.transpose(near, (1, 0, 2)).reshape(rank, total // 8)
        lifted = jnp.dot(l2l_ops[:, octant * rank:(octant + 1) * rank], far, precision=highest)
        spread = jnp.repeat(lifted, group, axis=1)
        outputs.append(near + spread)
    locals_out = jnp.transpose(jnp.stack(outputs), (1, 2, 0)).reshape(rank, total)
    return locals_out, parents
```

```python
import functools

import jax
import jax.numpy as jnp
from jax import lax
from jax.experimental import pallas as pl
from jax.experimental.pallas import tpu as pltpu
from jax.sharding import PartitionSpec as P

BF16 = jnp.bfloat16
F32 = jnp.float32
I32 = jnp.int32
MESH = pl.DeviceIdType.MESH
HIGHEST = lax.Precision.HIGHEST

DEVICES = 128
R = 48
K = 189
BOX = 384
CLASSES = 316
REACH = 7
RIM = 48
COARSE = 64
PARENTS = BOX // 8
GROUP = 96
BLOCKS = 2 * REACH
GROUPS = BLOCKS // 2
PAD_K = 192
CHUNKS = PAD_K // 4
FAR_ROWS = 64


def slot_of(distance):
    return distance + REACH if distance < 0 else distance + REACH - 1


DISTANCES = [s for a in range(1, REACH + 1) for s in (a, -a)]


def dot(a, b, precision=None):
    return jnp.dot(a, b, preferred_element_type=F32, precision=precision)


def dot_t(a, b, precision=None):
    return lax.dot_general(
        a, b, (((1,), (1,)), ((), ())), preferred_element_type=F32, precision=precision
    )


def iota(shape, dim):
    return lax.broadcasted_iota(I32, shape, dim)


def kernel(
    mult_hbm, part_hbm, off_hbm, cls_hbm, m2l_hbm, m2m_hbm, cops_hbm, coup_hbm, l2l_hbm,
    out_ref, par_ref,
    mult, part, off, cls, m2l, m2m, cops, coup, l2l,
    blk, rims, share, share_in, cbuf, lo_ref, hi_ref, strips, table, cube, gath, acc,
    in_sem, rim_send, rim_recv, pair_send, pair_recv, far_send, far_recv,
):
    me = lax.axis_index("box")
    chip = me // 2
    zc, yc, xc = chip % 4, (chip // 4) % 4, chip // 16
    core = me % 2

    loads = [
        pltpu.make_async_copy(src, dst, in_sem.at[i])
        for i, (src, dst) in enumerate(
            [
                (mult_hbm, mult), (m2m_hbm, m2m), (part_hbm, part), (off_hbm, off),
                (m2l_hbm, m2l), (cls_hbm.at[:, pl.ds(0, 128)], cls), (cops_hbm, cops),
                (coup_hbm, coup), (l2l_hbm, l2l),
            ]
        )
    ]
    for load in loads:
        load.start()

    def chip_peer(z, y, x):
        return ((x * 4 + y) * 4 + z) * 2 + core

    z_peers = [chip_peer((zc + m) % 4, yc, xc) for m in (1, 2, 3)]
    y_peers = [chip_peer(zc, (yc + m) % 4, xc) for m in (1, 2, 3)]
    x_peers = [chip_peer(zc, yc, (xc + m) % 4) for m in (1, 2, 3)]
    partner = me + 1 - 2 * core

    def valid(distance):
        return me + distance < DEVICES if distance > 0 else me + distance >= 0

    barrier = pltpu.get_barrier_semaphore()
    for distance in DISTANCES:
        @pl.when(valid(distance))
        def _():
            pl.semaphore_signal(
                barrier, inc=1, device_id=(me + distance,), device_id_type=MESH
            )
    for peer in y_peers + x_peers:
        pl.semaphore_signal(barrier, inc=1, device_id=(peer,), device_id_type=MESH)

    loads[0].wait()
    own = mult[...]
    own32 = own.astype(F32)
    lane = iota((R, 128), 1)
    upper = pltpu.roll(own32[:, 256:384], 96, 1)
    blk[...] = jnp.where(
        lane < RIM, own32[:, 0:128], jnp.where(lane < 2 * RIM, upper, 0.0)
    ).astype(BF16)

    expected = jnp.minimum(me, REACH) + jnp.minimum(DEVICES - 1 - me, REACH) + 6
    pl.semaphore_wait(barrier, expected)

    def rim_copy(distance):
        slot = slot_of(-distance)
        return pltpu.make_async_remote_copy(
            src_ref=blk,
            dst_ref=rims.at[slot],
            send_sem=rim_send.at[slot],
            recv_sem=rim_recv.at[slot],
            device_id=(me + distance,),
            device_id_type=MESH,
        )

    for distance in DISTANCES:
        @pl.when(valid(distance))
        def _():
            rim_copy(distance).start()

        @pl.when(jnp.logical_not(valid(distance)))
        def _():
            rims[slot_of(distance)] = jnp.zeros((R, 128), BF16)

    loads[1].wait()
    stacked = jnp.concatenate([m2m[:, R * j:R * j + R] for j in range(8)], axis=0)
    shifted = dot(stacked, own)
    octant = iota((R, BOX), 1) % 8
    mixed = jnp.zeros((R, BOX), F32)
    for j in range(8):
        mixed = jnp.where(octant == j, shifted[R * j:R * j + R], mixed)
    pool = (iota((BOX, PARENTS), 0) // 8 == iota((BOX, PARENTS), 1)).astype(F32)
    parents = dot(mixed, pool, HIGHEST)
    par_ref[...] = parents
    ones = jnp.ones((8, PARENTS), F32)
    total = dot_t(ones, parents, HIGHEST) * jnp.float32(GROUP ** (-0.5))
    share[...] = jnp.zeros((1, 128), F32)
    share[:, 0:R] = total[0:1, :]
    pair = pltpu.make_async_remote_copy(
        src_ref=share, dst_ref=share_in, send_sem=pair_send, recv_sem=pair_recv,
        device_id=(partner,), device_id_type=MESH,
    )
    pair.start()

    for i in range(BLOCKS):
        if i < BOX // 32:
            piece = own32[:, 128 * (i // 4):128 * (i // 4) + 128]
            shift = (96 - 32 * (i % 4)) % 128
            if shift:
                piece = pltpu.roll(piece, shift, 1)
            strips[i] = jnp.where(lane >= 2 * RIM, piece, 0.0).astype(BF16)
        else:
            strips[i] = jnp.zeros((R, 128), BF16)

    loads[2].wait()
    loads[3].wait()
    lo_ref[...] = jnp.zeros((PAD_K, BOX), F32)
    hi_ref[...] = jnp.full((PAD_K, BOX), GROUPS, I32)
    within, half = part[...], off[...]
    second = half & 1
    pos = half >> 1
    here = pos == REACH
    local = within + 192 * second
    local_col = ((local >> 5) << 7) + 96 + (local & 31)
    block = jnp.where(pos > REACH, pos - 1, pos)
    remote_col = (block << 7) + within + second * (RIM - 144)
    col = jnp.where(here, local_col, remote_col)
    lo_ref[0:K, :] = (col & 255).astype(F32)
    hi_ref[0:K, :] = col >> 8

    loads[4].wait()
    row, column = iota((256, 512), 0), iota((256, 512), 1)
    inner = column & 63
    start = R * (column >> 7)
    live = inner < R
    first = jnp.where(live & (row == start + inner), 1.0, 0.0).astype(BF16)
    second_half = jnp.where(live & (row == start + 64 + inner), 1.0, 0.0).astype(BF16)

    def spread(step, _):
        tops, bottoms = [], []
        for u in range(3):
            base = pl.multiple_of((step * 3 + u) * 384, 128)
            tops.append(m2l[:, pl.ds(base, 256)])
            bottoms.append(m2l[:, pl.ds(pl.multiple_of(base + 128, 128), 256)])
        a = dot(jnp.concatenate(tops, axis=0), first).astype(BF16)
        b = dot(jnp.concatenate(bottoms, axis=0), second_half).astype(BF16)
        for u in range(3):
            for j in range(4):
                cube[(step * 3 + u) * 8 + j] = a[R * u:R * u + R, 128 * j:128 * j + 128]
                cube[(step * 3 + u) * 8 + 4 + j] = b[R * u:R * u + R, 128 * j:128 * j + 128]
        return 0

    lax.fori_loop(0, 13, spread, 0)
    tail = dot(m2l[:, 39 * 384:CLASSES * R], first[0:192, :]).astype(BF16)
    for j in range(4):
        cube[312 + j] = tail[:, 128 * j:128 * j + 128]

    def clear(step, _):
        for q in range(4):
            at = pl.multiple_of(step * 256 + 64 * q + R, 16)
            gath[pl.ds(at, 16), :] = jnp.zeros((16, BOX), BF16)
        return 0

    lax.fori_loop(0, CHUNKS, clear, 0)

    pair.wait()
    cbuf[chip] = share[...] + share_in[...]

    def far_copies(stage, peers, start, count):
        return [
            pltpu.make_async_remote_copy(
                src_ref=cbuf.at[pl.ds(start, count)],
                dst_ref=cbuf.at[pl.ds(start, count)],
                send_sem=far_send.at[stage, m],
                recv_sem=far_recv.at[stage, m],
                device_id=(peer,),
                device_id_type=MESH,
            )
            for m, peer in enumerate(peers)
        ]

    along_z = far_copies(0, z_peers, chip, 1)
    along_y = far_copies(1, y_peers, (chip // 4) * 4, 4)
    along_x = far_copies(2, x_peers, (chip // 16) * 16, 16)
    for copy in along_z:
        copy.start()

    for distance in DISTANCES:
        @pl.when(valid(distance))
        def _():
            rim_copy(-distance).wait_recv()
    for i in range(BLOCKS):
        g, side = i // 2, i % 2
        table[R * g:R * g + R, 128 * side:128 * side + 128] = jnp.where(
            lane < 2 * RIM, rims[i].astype(F32), strips[i].astype(F32)
        ).astype(BF16)

    index = iota((256, 128), 0).astype(F32).astype(BF16)

    def one_hot(lo, k):
        pieces = []
        for j in range(3):
            wanted = jnp.broadcast_to(lo[k:k + 1, 128 * j:128 * j + 128], (256, 128))
            pieces.append(
                jnp.where(wanted.astype(BF16) == index, jnp.ones((), BF16), jnp.zeros((), BF16))
            )
        return jnp.concatenate(pieces, axis=1)

    def gather(step, _):
        base = pl.multiple_of(step * 16, 16)
        lo = lo_ref[pl.ds(base, 16), :]
        hi = hi_ref[pl.ds(base, 16), :]
        for p in range(0, 16, 2):
            hot = jnp.concatenate([one_hot(lo, p), one_hot(lo, p + 1)], axis=1)
            found = dot(table[...], hot)
            for q in range(2):
                wanted = jnp.broadcast_to(hi[p + q:p + q + 1, :], (R, BOX))
                value = jnp.zeros((R, BOX), F32)
                for g in range(GROUPS):
                    part_of = found[R * g:R * g + R, BOX * q:BOX * q + BOX]
                    value = jnp.where(wanted == g, part_of, value)
                at = pl.multiple_of(step * 1024 + 64 * (p + q), 64)
                gath[pl.ds(at, R), :] = value.astype(BF16)
        return 0

    lax.fori_loop(0, 4, gather, 0)
    for copy in along_z:
        copy.wait()
    for copy in along_y:
        copy.start()
    lax.fori_loop(4, 8, gather, 0)
    for copy in along_y:
        copy.wait()
    for copy in along_x:
        copy.start()
    lax.fori_loop(8, 12, gather, 0)
    for copy in along_x:
        copy.wait()

    for load in loads[6:9]:
        load.wait()
    coarse = cbuf[...].reshape(COARSE, 128)
    mixed_far = dot(coup[...], coarse, HIGHEST)
    mine = jnp.sum(
        jnp.where(iota((COARSE, 128), 0) == chip, mixed_far, 0.0), axis=0, keepdims=True
    )
    far = dot_t(jnp.broadcast_to(mine[:, 0:R], (8, R)), cops[...], HIGHEST)
    tile = (iota((R, BOX), 1) % R == iota((R, BOX), 0)).astype(F32)
    far_tiled = dot(far, tile, HIGHEST)
    terms = l2l[...] * far_tiled[0:1, :]
    by_octant = (iota((BOX, BOX), 0) // R == iota((BOX, BOX), 1) % 8).astype(F32)
    lifted = dot(terms, by_octant, HIGHEST)

    loads[5].wait()
    acc[...] = jnp.zeros(acc.shape, F32)
    lower = iota((R, 128), 1).astype(F32).astype(BF16) < jnp.full((), 64, BF16)

    def translate(step, _):
        lhs = []
        for o in range(8):
            pairs = []
            for q in range(0, 8, 2):
                k0 = jnp.minimum(step * 8 + q, K - 1)
                k1 = jnp.minimum(step * 8 + q + 1, K - 1)
                pairs.append(jnp.where(lower, cube[cls[k0, o]], cube[cls[k1, o]]))
            lhs.append(jnp.concatenate(pairs, axis=1))
        at = pl.multiple_of(step * 512, 512)
        acc[...] += dot(jnp.concatenate(lhs, axis=0), gath[pl.ds(at, 512), :])
        return 0

    lax.fori_loop(0, CHUNKS // 2, translate, 0)
    near = jnp.zeros((R, BOX), F32)
    for o in range(8):
        near = jnp.where(octant == o, acc[R * o:R * o + R, :], near)
    out_ref[...] = near + lifted

    for distance in DISTANCES:
        @pl.when(valid(distance))
        def _():
            rim_copy(distance).wait_send()


def shards(multipoles, partners, partner_offset, classes, m2l_ops, m2m_ops, coarse_ops, coupling, l2l_ops):
    any_space = pl.BlockSpec(memory_space=pl.ANY)
    vmem = pl.BlockSpec(memory_space=pltpu.VMEM)
    dma = pltpu.SemaphoreType.DMA
    return pl.pallas_call(
        kernel,
        name="far_field",
        out_shape=(
            jax.ShapeDtypeStruct((R, BOX), F32),
            jax.ShapeDtypeStruct((R, PARENTS), F32),
        ),
        in_specs=[any_space] * 9,
        out_specs=(vmem, vmem),
        scratch_shapes=[
            pltpu.VMEM((R, BOX), BF16),
            pltpu.VMEM((K, BOX), I32),
            pltpu.VMEM((K, BOX), I32),
            pltpu.SMEM((K, 128), I32),
            pltpu.VMEM((R, CLASSES * R), BF16),
            pltpu.VMEM((R, 8 * R), BF16),
            pltpu.VMEM((R, R), F32),
            pltpu.VMEM((COARSE, COARSE), F32),
            pltpu.VMEM((R, 8 * R), F32),
            pltpu.VMEM((R, 128), BF16),
            pltpu.VMEM((BLOCKS, R, 128), BF16),
            pltpu.VMEM((1, 128), F32),
            pltpu.VMEM((1, 128), F32),
            pltpu.VMEM((COARSE, 1, 128), F32),
            pltpu.VMEM((PAD_K, BOX), F32),
            pltpu.VMEM((PAD_K, BOX), I32),
            pltpu.VMEM((BLOCKS, R, 128), BF16),
            pltpu.VMEM((GROUPS * R, 256), BF16),
            pltpu.VMEM((CLASSES, R, 128), BF16),
            pltpu.VMEM((PAD_K * 64, BOX), BF16),
            pltpu.VMEM((8 * R, BOX), F32),
            dma((9,)),
            dma((BLOCKS,)),
            dma((BLOCKS,)),
            dma,
            dma,
            dma((3, 3)),
            dma((3, 3)),
        ],
        compiler_params=pltpu.CompilerParams(
            collective_id=0, has_side_effects=True, vmem_limit_bytes=48 * 1024 * 1024
        ),
    )(multipoles, partners, partner_offset, classes, m2l_ops, m2m_ops, coarse_ops, coupling, l2l_ops)


def solution(mesh):
    placed = (
        P(None, "box"), P(None, "box"), P(None, "box"), P(None, "box"),
        P(), P(), P(), P(), P(),
    )
    return jax.shard_map(
        shards,
        mesh=mesh,
        in_specs=placed,
        out_specs=(P(None, "box"), P(None, "box")),
        check_vma=False,
    )
```

```python
import functools

import jax
import jax.numpy as jnp
from jax import lax
from jax.experimental import pallas as pl
from jax.experimental.pallas import tpu as pltpu
from jax.sharding import PartitionSpec as P

BF16 = jnp.bfloat16
F32 = jnp.float32
I32 = jnp.int32
MESH = pl.DeviceIdType.MESH
HIGHEST = lax.Precision.HIGHEST

DEVICES = 128
R = 48
K = 189
BOX = 384
CLASSES = 316
REACH = 7
RIM = 48
COARSE = 64
PARENTS = BOX // 8
GROUP = 96
BLOCKS = 2 * REACH
GROUPS = BLOCKS // 2
PAD_K = 190
CHUNKS = PAD_K // 5
STEPS = CHUNKS // 2
LANE_SLOTS = (4, 9)
PRODUCT_SLOTS = ((0, 1), (2, 3), (5, 6), (7, 8))
PLACES = (
    ((0, 0, 48),), ((48, 0, 48),), ((96, 0, 32), (240, 32, 16)), ((128, 0, 48),), ((176, 0, 48),),
)


def slot_of(distance):
    return distance + REACH if distance < 0 else distance + REACH - 1


DISTANCES = [s for a in range(1, REACH + 1) for s in (a, -a)]


def dot(a, b, precision=None):
    return jnp.dot(a, b, preferred_element_type=F32, precision=precision)


def dot_t(a, b, precision=None):
    return lax.dot_general(
        a, b, (((1,), (1,)), ((), ())), preferred_element_type=F32, precision=precision
    )


def iota(shape, dim):
    return lax.broadcasted_iota(I32, shape, dim)


def lanes_from(x, source):
    tiles = []
    for v in range(3):
        wanted = source[:, 128 * v:128 * v + 128]
        inside, tile = wanted & 127, wanted >> 7
        found = None
        for u in range(3):
            moved = jnp.take_along_axis(
                x[:, 128 * u:128 * u + 128], inside, axis=1, mode="promise_in_bounds"
            )
            found = moved if u == 0 else jnp.where(tile == u, moved, found)
        tiles.append(found)
    return jnp.concatenate(tiles, axis=1)


def kernel(
    mult_hbm, part_hbm, off_hbm, cls_hbm, m2l_hbm, m2m_hbm, cops_hbm, coup_hbm, l2l_hbm,
    out_ref, par_ref,
    mult, part, off, cls, m2l, m2m, cops, coup, l2l,
    blk, rims, share, share_in, cbuf, cols, cols_ref, lo_ref, hi_ref, strips, table, wide, cube, gath, acc_a, acc_b,
    in_sem, rim_send, rim_recv, pair_send, pair_recv, far_send, far_recv,
):
    me = lax.axis_index("box")
    chip = me // 2
    zc, yc, xc = chip % 4, (chip // 4) % 4, chip // 16
    core = me % 2

    loads = [
        pltpu.make_async_copy(src, dst, in_sem.at[i])
        for i, (src, dst) in enumerate(
            [
                (mult_hbm, mult), (m2m_hbm, m2m), (part_hbm, part), (off_hbm, off),
                (m2l_hbm, m2l), (cls_hbm.at[:, pl.ds(0, 128)], cls), (cops_hbm, cops),
                (coup_hbm, coup), (l2l_hbm, l2l),
            ]
        )
    ]
    for load in loads:
        load.start()

    def chip_peer(z, y, x):
        return ((x * 4 + y) * 4 + z) * 2 + core

    z_peers = [chip_peer((zc + m) % 4, yc, xc) for m in (1, 2, 3)]
    y_peers = [chip_peer(zc, (yc + m) % 4, xc) for m in (1, 2, 3)]
    x_peers = [chip_peer(zc, yc, (xc + m) % 4) for m in (1, 2, 3)]
    partner = me + 1 - 2 * core

    def valid(distance):
        return me + distance < DEVICES if distance > 0 else me + distance >= 0

    barrier = pltpu.get_barrier_semaphore()
    for distance in DISTANCES:
        @pl.when(valid(distance))
        def _():
            pl.semaphore_signal(
                barrier, inc=1, device_id=(me + distance,), device_id_type=MESH
            )
    for peer in y_peers + x_peers:
        pl.semaphore_signal(barrier, inc=1, device_id=(peer,), device_id_type=MESH)

    loads[0].wait()
    own = mult[...]
    own32 = own.astype(F32)
    lane = iota((R, 128), 1)
    upper = pltpu.roll(own32[:, 256:384], 96, 1)
    blk[...] = jnp.where(
        lane < RIM, own32[:, 0:128], jnp.where(lane < 2 * RIM, upper, 0.0)
    ).astype(BF16)

    for i in range(BLOCKS):
        if i < BOX // 32:
            piece = own32[:, 128 * (i // 4):128 * (i // 4) + 128]
            shift = (96 - 32 * (i % 4)) % 128
            if shift:
                piece = pltpu.roll(piece, shift, 1)
            strips[i] = jnp.where(lane >= 2 * RIM, piece, 0.0).astype(BF16)
        else:
            strips[i] = jnp.zeros((R, 128), BF16)

    loads[2].wait()
    loads[3].wait()
    within, half = part[...], off[...]
    second = half & 1
    pos = half >> 1
    here = pos == REACH
    local = within + 192 * second
    local_col = ((local >> 5) << 7) + 96 + (local & 31)
    block = jnp.where(pos > REACH, pos - 1, pos)
    remote_col = (block << 7) + within + second * (RIM - 144)
    col = jnp.where(here, local_col, remote_col)
    cols[...] = jnp.full((192, BOX), 256 * GROUPS, I32)
    cols[0:K, :] = col
    slot = iota((192, BOX), 1)
    col = lanes_from(cols[...], 8 * (slot % PARENTS) + slot // PARENTS)
    cols_ref[...] = col
    lo_ref[...] = (col & 255).astype(F32)
    hi_ref[...] = col >> 8

    expected = jnp.minimum(me, REACH) + jnp.minimum(DEVICES - 1 - me, REACH) + 6
    pl.semaphore_wait(barrier, expected)

    def rim_copy(distance):
        slot = slot_of(-distance)
        return pltpu.make_async_remote_copy(
            src_ref=blk,
            dst_ref=rims.at[slot],
            send_sem=rim_send.at[slot],
            recv_sem=rim_recv.at[slot],
            device_id=(me + distance,),
            device_id_type=MESH,
        )

    for distance in DISTANCES:
        @pl.when(valid(distance))
        def _():
            rim_copy(distance).start()

        @pl.when(jnp.logical_not(valid(distance)))
        def _():
            rims[slot_of(distance)] = jnp.zeros((R, 128), BF16)

    loads[1].wait()
    stacked = jnp.concatenate([m2m[:, R * j:R * j + R] for j in range(8)], axis=0)
    shifted = dot(stacked, own)
    octant = iota((R, BOX), 1) % 8
    mixed = jnp.zeros((R, BOX), F32)
    for j in range(8):
        mixed = jnp.where(octant == j, shifted[R * j:R * j + R], mixed)
    pool = (iota((BOX, PARENTS), 0) // 8 == iota((BOX, PARENTS), 1)).astype(F32)
    parents = dot(mixed, pool, HIGHEST)
    par_ref[...] = parents
    ones = jnp.ones((8, PARENTS), F32)
    total = dot_t(ones, parents, HIGHEST) * jnp.float32(GROUP ** (-0.5))
    share[...] = jnp.zeros((1, 128), F32)
    share[:, 0:R] = total[0:1, :]
    pair = pltpu.make_async_remote_copy(
        src_ref=share, dst_ref=share_in, send_sem=pair_send, recv_sem=pair_recv,
        device_id=(partner,), device_id_type=MESH,
    )
    pair.start()

    loads[4].wait()
    row, column = iota((256, 512), 0), iota((256, 512), 1)
    wanted = R * (column >> 7) + (column & 127) % R
    first = jnp.where(row == wanted, 1.0, 0.0).astype(BF16)
    second_half = jnp.where(row == wanted + 64, 1.0, 0.0).astype(BF16)

    def spread(step, _):
        tops, bottoms = [], []
        for u in range(3):
            base = pl.multiple_of((step * 3 + u) * 384, 128)
            tops.append(m2l[:, pl.ds(base, 256)])
            bottoms.append(m2l[:, pl.ds(pl.multiple_of(base + 128, 128), 256)])
        a = dot(jnp.concatenate(tops, axis=0), first).astype(BF16)
        b = dot(jnp.concatenate(bottoms, axis=0), second_half).astype(BF16)
        for u in range(3):
            for j in range(4):
                cube[(step * 3 + u) * 8 + j] = a[R * u:R * u + R, 128 * j:128 * j + 128]
                cube[(step * 3 + u) * 8 + 4 + j] = b[R * u:R * u + R, 128 * j:128 * j + 128]
        return 0

    lax.fori_loop(0, 13, spread, 0)
    tail = dot(m2l[:, 39 * 384:CLASSES * R], first[0:192, :]).astype(BF16)
    for j in range(4):
        cube[312 + j] = tail[:, 128 * j:128 * j + 128]

    def clear(step, _):
        at = pl.multiple_of(step * 256 + 224, 16)
        gath[pl.ds(at, 16), :] = jnp.zeros((16, BOX), BF16)
        return 0

    lax.fori_loop(2, CHUNKS + 2, clear, 0)
    gath[0:512, :] = jnp.zeros((512, BOX), BF16)

    pair.wait()
    cbuf[chip] = share[...] + share_in[...]

    def far_copies(stage, peers, start, count):
        return [
            pltpu.make_async_remote_copy(
                src_ref=cbuf.at[pl.ds(start, count)],
                dst_ref=cbuf.at[pl.ds(start, count)],
                send_sem=far_send.at[stage, m],
                recv_sem=far_recv.at[stage, m],
                device_id=(peer,),
                device_id_type=MESH,
            )
            for m, peer in enumerate(peers)
        ]

    along_z = far_copies(0, z_peers, chip, 1)
    along_y = far_copies(1, y_peers, (chip // 4) * 4, 4)
    along_x = far_copies(2, x_peers, (chip // 16) * 16, 16)
    for copy in along_z:
        copy.start()

    for distance in DISTANCES:
        @pl.when(valid(distance))
        def _():
            rim_copy(-distance).wait_recv()
    for i in range(BLOCKS):
        g, side = i // 2, i % 2
        columns = jnp.where(lane < 2 * RIM, rims[i].astype(F32), strips[i].astype(F32))
        wide[i] = columns
        table[R * g:R * g + R, 128 * side:128 * side + 128] = columns.astype(BF16)

    index = iota((256, 128), 0).astype(F32).astype(BF16)

    def one_hot(lo, k):
        pieces = []
        for j in range(3):
            wanted = jnp.broadcast_to(lo[k:k + 1, 128 * j:128 * j + 128], (256, 128))
            pieces.append(
                jnp.where(wanted.astype(BF16) == index, jnp.ones((), BF16), jnp.zeros((), BF16))
            )
        return jnp.concatenate(pieces, axis=1)

    def keep(step, p, value):
        for to, start, count in PLACES[p % 5]:
            at = pl.multiple_of(step * 512 + 512 + 256 * (p // 5) + to, 16)
            gath[pl.ds(at, count), :] = value[start:start + count]

    def gather(step):
        for p in LANE_SLOTS:
            tiles = []
            sought = cols_ref[pl.ds(step * 10 + p, 1), :]
            for v in range(3):
                wanted = jnp.broadcast_to(sought[:, 128 * v:128 * v + 128], (R, 128))
                inside, tile = wanted & 127, wanted >> 7
                value = jnp.zeros((R, 128), F32)
                for i in range(BLOCKS):
                    moved = jnp.take_along_axis(wide[i], inside, axis=1, mode="promise_in_bounds")
                    value = jnp.where(tile == i, moved, value)
                tiles.append(value.astype(BF16))
            keep(step, p, jnp.concatenate(tiles, axis=1))
        for pair_of in PRODUCT_SLOTS:
            lo = [lo_ref[pl.ds(step * 10 + p, 1), :] for p in pair_of]
            hi = [hi_ref[pl.ds(step * 10 + p, 1), :] for p in pair_of]
            hot = jnp.concatenate([one_hot(x, 0) for x in lo], axis=1)
            found = dot(table[...], hot)
            for q, p in enumerate(pair_of):
                wanted = jnp.broadcast_to(hi[q], (R, BOX))
                value = jnp.zeros((R, BOX), F32)
                for g in range(GROUPS):
                    part_of = found[R * g:R * g + R, BOX * q:BOX * q + BOX]
                    value = jnp.where(wanted == g, part_of, value)
                keep(step, p, value.astype(BF16))

    loads[5].wait()
    acc_a[...] = jnp.zeros(acc_a.shape, F32)
    acc_b[...] = jnp.zeros(acc_b.shape, F32)
    at_lane = iota((R, 128), 1).astype(F32).astype(BF16)
    below_48 = at_lane < jnp.full((), 48, BF16)
    below_96 = at_lane < jnp.full((), 96, BF16)

    def translate(step, last):
        first_slot = 10 * jnp.maximum(step - 1, 0)
        lhs = []
        for o in range(8):
            tiles = []
            for chunk in range(2):
                ops = []
                for q in range(5):
                    k = first_slot + 5 * chunk + q
                    if last and chunk and q == 4:
                        k = jnp.minimum(k, K - 1)
                    ops.append(cube[cls[k, o]])
                tiles.append(jnp.where(below_48, ops[0], jnp.where(below_96, ops[1], ops[2])))
                rest = pltpu.roll(ops[2], 32, 1)
                tiles.append(jnp.where(below_48, ops[3], jnp.where(below_96, ops[4], rest)))
            lhs.append(jnp.concatenate(tiles, axis=1))
        at = pl.multiple_of(step * 512, 512)
        acc_a[...] += dot(jnp.concatenate(lhs[0:6], axis=0), gath[pl.ds(at, 512), 0:256])
        acc_b[...] += dot(jnp.concatenate(lhs[5:8], axis=0), gath[pl.ds(at, 512), 256:384])

    def both(step, _):
        translate(step, False)
        gather(step)
        return 0

    lax.fori_loop(0, 6, both, 0)
    for copy in along_z:
        copy.wait()
    for copy in along_y:
        copy.start()
    lax.fori_loop(6, 12, both, 0)
    for copy in along_y:
        copy.wait()
    for copy in along_x:
        copy.start()
    lax.fori_loop(12, STEPS, both, 0)
    for copy in along_x:
        copy.wait()

    for load in loads[6:9]:
        load.wait()
    coarse = cbuf[...].reshape(COARSE, 128)
    mixed_far = dot(coup[...], coarse, HIGHEST)
    mine = jnp.sum(
        jnp.where(iota((COARSE, 128), 0) == chip, mixed_far, 0.0), axis=0, keepdims=True
    )
    far = dot_t(jnp.broadcast_to(mine[:, 0:R], (8, R)), cops[...], HIGHEST)
    tile = (iota((R, BOX), 1) % R == iota((R, BOX), 0)).astype(F32)
    far_tiled = dot(far, tile, HIGHEST)
    terms = l2l[...] * far_tiled[0:1, :]
    by_octant = (iota((BOX, BOX), 0) // R == iota((BOX, BOX), 1) // PARENTS).astype(F32)
    lifted = dot(terms, by_octant, HIGHEST)

    translate(STEPS, True)
    left_octant = iota((R, 256), 1) // PARENTS
    right_octant = (iota((R, 128), 1) + 256) // PARENTS
    left, right = acc_a[0:R, :], acc_b[0:R, :]
    for o in range(1, 6):
        left = jnp.where(left_octant == o, acc_a[R * o:R * o + R, :], left)
    for o in (6, 7):
        right = jnp.where(right_octant == o, acc_b[R * (o - 5):R * (o - 5) + R, :], right)
    sums = jnp.concatenate([left, right], axis=1) + lifted
    box = iota((R, BOX), 1)
    out_ref[...] = lanes_from(sums, PARENTS * (box % 8) + box // 8)

    for distance in DISTANCES:
        @pl.when(valid(distance))
        def _():
            rim_copy(distance).wait_send()


def shards(multipoles, partners, partner_offset, classes, m2l_ops, m2m_ops, coarse_ops, coupling, l2l_ops):
    any_space = pl.BlockSpec(memory_space=pl.ANY)
    vmem = pl.BlockSpec(memory_space=pltpu.VMEM)
    dma = pltpu.SemaphoreType.DMA
    return pl.pallas_call(
        kernel,
        name="far_field",
        out_shape=(
            jax.ShapeDtypeStruct((R, BOX), F32),
            jax.ShapeDtypeStruct((R, PARENTS), F32),
        ),
        in_specs=[any_space] * 9,
        out_specs=(vmem, vmem),
        scratch_shapes=[
            pltpu.VMEM((R, BOX), BF16),
            pltpu.VMEM((K, BOX), I32),
            pltpu.VMEM((K, BOX), I32),
            pltpu.SMEM((K, 128), I32),
            pltpu.VMEM((R, CLASSES * R), BF16),
            pltpu.VMEM((R, 8 * R), BF16),
            pltpu.VMEM((R, R), F32),
            pltpu.VMEM((COARSE, COARSE), F32),
            pltpu.VMEM((R, 8 * R), F32),
            pltpu.VMEM((R, 128), BF16),
            pltpu.VMEM((BLOCKS, R, 128), BF16),
            pltpu.VMEM((1, 128), F32),
            pltpu.VMEM((1, 128), F32),
            pltpu.VMEM((COARSE, 1, 128), F32),
            pltpu.VMEM((192, BOX), I32),
            pltpu.VMEM((192, BOX), I32),
            pltpu.VMEM((192, BOX), F32),
            pltpu.VMEM((192, BOX), I32),
            pltpu.VMEM((BLOCKS, R, 128), BF16),
            pltpu.VMEM((GROUPS * R, 256), BF16),
            pltpu.VMEM((BLOCKS, R, 128), F32),
            pltpu.VMEM((CLASSES, R, 128), BF16),
            pltpu.VMEM(((CHUNKS + 2) * 256, BOX), BF16),
            pltpu.VMEM((6 * R, 256), F32),
            pltpu.VMEM((3 * R, 128), F32),
            dma((9,)),
            dma((BLOCKS,)),
            dma((BLOCKS,)),
            dma,
            dma,
            dma((3, 3)),
            dma((3, 3)),
        ],
        compiler_params=pltpu.CompilerParams(
            collective_id=0, has_side_effects=True, vmem_limit_bytes=62 * 1024 * 1024
        ),
    )(multipoles, partners, partner_offset, classes, m2l_ops, m2m_ops, coarse_ops, coupling, l2l_ops)


def solution(mesh):
    placed = (
        P(None, "box"), P(None, "box"), P(None, "box"), P(None, "box"),
        P(), P(), P(), P(), P(),
    )
    return jax.shard_map(
        shards,
        mesh=mesh,
        in_specs=placed,
        out_specs=(P(None, "box"), P(None, "box")),
        check_vma=False,
    )
```

```python
import functools

import jax
import jax.numpy as jnp
from jax import lax
from jax.experimental import pallas as pl
from jax.experimental.pallas import tpu as pltpu
from jax.sharding import PartitionSpec as P

BF16 = jnp.bfloat16
F32 = jnp.float32
I32 = jnp.int32
MESH = pl.DeviceIdType.MESH
HIGHEST = lax.Precision.HIGHEST

DEVICES = 128
R = 48
K = 189
BOX = 384
CLASSES = 316
REACH = 7
RIM = 48
COARSE = 64
PARENTS = BOX // 8
GROUP = 96
BLOCKS = 2 * REACH
GROUPS = BLOCKS // 2
PAD_K = 190
CHUNKS = PAD_K // 5
STEPS = CHUNKS // 2
LANE_SLOTS = (4, 9)
PRODUCT_SLOTS = ((0, 1), (2, 3), (5, 6), (7, 8))
PLACES = (
    ((0, 0, 48),), ((48, 0, 48),), ((96, 0, 32), (240, 32, 16)), ((128, 0, 48),), ((176, 0, 48),),
)


def slot_of(distance):
    return distance + REACH if distance < 0 else distance + REACH - 1


DISTANCES = [s for a in range(1, REACH + 1) for s in (a, -a)]


def dot(a, b, precision=None):
    return jnp.dot(a, b, preferred_element_type=F32, precision=precision)


def dot_t(a, b, precision=None):
    return lax.dot_general(
        a, b, (((1,), (1,)), ((), ())), preferred_element_type=F32, precision=precision
    )


def iota(shape, dim):
    return lax.broadcasted_iota(I32, shape, dim)


def lanes_from(x, source):
    tiles = []
    for v in range(3):
        wanted = source[:, 128 * v:128 * v + 128]
        inside, tile = wanted & 127, wanted >> 7
        found = None
        for u in range(3):
            moved = jnp.take_along_axis(
                x[:, 128 * u:128 * u + 128], inside, axis=1, mode="promise_in_bounds"
            )
            found = moved if u == 0 else jnp.where(tile == u, moved, found)
        tiles.append(found)
    return jnp.concatenate(tiles, axis=1)


def kernel(
    mult_hbm, part_hbm, off_hbm, cls_hbm, m2l_hbm, m2m_hbm, cops_hbm, coup_hbm, l2l_hbm,
    out_ref, par_ref,
    mult, part, off, cls, m2l, m2m, cops, coup, l2l,
    blk, rims, share, share_in, cbuf, cols, cols_ref, lo_ref, hi_ref, strips, table, wide, cube, even, odd, acc_a, acc_b,
    in_sem, rim_send, rim_recv, pair_send, pair_recv, far_send, far_recv,
):
    me = lax.axis_index("box")
    chip = me // 2
    zc, yc, xc = chip % 4, (chip // 4) % 4, chip // 16
    core = me % 2

    loads = [
        pltpu.make_async_copy(src, dst, in_sem.at[i])
        for i, (src, dst) in enumerate(
            [
                (mult_hbm, mult), (m2m_hbm, m2m), (part_hbm, part), (off_hbm, off),
                (m2l_hbm, m2l), (cls_hbm.at[:, pl.ds(0, 128)], cls), (cops_hbm, cops),
                (coup_hbm, coup), (l2l_hbm, l2l),
            ]
        )
    ]
    for load in loads:
        load.start()

    def chip_peer(z, y, x):
        return ((x * 4 + y) * 4 + z) * 2 + core

    z_peers = [chip_peer((zc + m) % 4, yc, xc) for m in (1, 2, 3)]
    y_peers = [chip_peer(zc, (yc + m) % 4, xc) for m in (1, 2, 3)]
    x_peers = [chip_peer(zc, yc, (xc + m) % 4) for m in (1, 2, 3)]
    partner = me + 1 - 2 * core

    def valid(distance):
        return me + distance < DEVICES if distance > 0 else me + distance >= 0

    barrier = pltpu.get_barrier_semaphore()
    for distance in DISTANCES:
        @pl.when(valid(distance))
        def _():
            pl.semaphore_signal(
                barrier, inc=1, device_id=(me + distance,), device_id_type=MESH
            )
    for peer in y_peers + x_peers:
        pl.semaphore_signal(barrier, inc=1, device_id=(peer,), device_id_type=MESH)

    loads[0].wait()
    own = mult[...]
    own32 = own.astype(F32)
    lane = iota((R, 128), 1)
    upper = pltpu.roll(own32[:, 256:384], 96, 1)
    blk[...] = jnp.where(
        lane < RIM, own32[:, 0:128], jnp.where(lane < 2 * RIM, upper, 0.0)
    ).astype(BF16)

    for i in range(BLOCKS):
        if i < BOX // 32:
            piece = own32[:, 128 * (i // 4):128 * (i // 4) + 128]
            shift = (96 - 32 * (i % 4)) % 128
            if shift:
                piece = pltpu.roll(piece, shift, 1)
            strips[i] = jnp.where(lane >= 2 * RIM, piece, 0.0).astype(BF16)
        else:
            strips[i] = jnp.zeros((R, 128), BF16)

    loads[2].wait()
    loads[3].wait()
    within, half = part[...], off[...]
    second = half & 1
    pos = half >> 1
    here = pos == REACH
    local = within + 192 * second
    local_col = ((local >> 5) << 7) + 96 + (local & 31)
    block = jnp.where(pos > REACH, pos - 1, pos)
    remote_col = (block << 7) + within + second * (RIM - 144)
    col = jnp.where(here, local_col, remote_col)
    cols[...] = jnp.full((192, BOX), 256 * GROUPS, I32)
    cols[0:K, :] = col
    slot = iota((192, BOX), 1)
    col = lanes_from(cols[...], 8 * (slot % PARENTS) + slot // PARENTS)
    cols_ref[...] = col
    lo_ref[...] = (col & 255).astype(F32)
    hi_ref[...] = col >> 8

    expected = jnp.minimum(me, REACH) + jnp.minimum(DEVICES - 1 - me, REACH) + 6
    pl.semaphore_wait(barrier, expected)

    def rim_copy(distance):
        slot = slot_of(-distance)
        return pltpu.make_async_remote_copy(
            src_ref=blk,
            dst_ref=rims.at[slot],
            send_sem=rim_send.at[slot],
            recv_sem=rim_recv.at[slot],
            device_id=(me + distance,),
            device_id_type=MESH,
        )

    for distance in DISTANCES:
        @pl.when(valid(distance))
        def _():
            rim_copy(distance).start()

        @pl.when(jnp.logical_not(valid(distance)))
        def _():
            rims[slot_of(distance)] = jnp.zeros((R, 128), BF16)

    loads[1].wait()
    stacked = jnp.concatenate([m2m[:, R * j:R * j + R] for j in range(8)], axis=0)
    shifted = dot(stacked, own)
    octant = iota((R, BOX), 1) % 8
    mixed = jnp.zeros((R, BOX), F32)
    for j in range(8):
        mixed = jnp.where(octant == j, shifted[R * j:R * j + R], mixed)
    pool = (iota((BOX, PARENTS), 0) // 8 == iota((BOX, PARENTS), 1)).astype(F32)
    parents = dot(mixed, pool, HIGHEST)
    par_ref[...] = parents
    ones = jnp.ones((8, PARENTS), F32)
    total = dot_t(ones, parents, HIGHEST) * jnp.float32(GROUP ** (-0.5))
    share[...] = jnp.zeros((1, 128), F32)
    share[:, 0:R] = total[0:1, :]
    pair = pltpu.make_async_remote_copy(
        src_ref=share, dst_ref=share_in, send_sem=pair_send, recv_sem=pair_recv,
        device_id=(partner,), device_id_type=MESH,
    )
    pair.start()

    loads[4].wait()
    row, column = iota((256, 512), 0), iota((256, 512), 1)
    wanted = R * (column >> 7) + (column & 127) % R
    first = jnp.where(row == wanted, 1.0, 0.0).astype(BF16)
    second_half = jnp.concatenate([jnp.zeros((64, 512), BF16), first[0:192]], axis=0)

    def spread(step, _):
        tops, bottoms = [], []
        for u in range(3):
            base = pl.multiple_of((step * 3 + u) * 384, 128)
            tops.append(m2l[:, pl.ds(base, 256)])
            bottoms.append(m2l[:, pl.ds(pl.multiple_of(base + 128, 128), 256)])
        a = dot(jnp.concatenate(tops, axis=0), first).astype(BF16)
        b = dot(jnp.concatenate(bottoms, axis=0), second_half).astype(BF16)
        for u in range(3):
            for j in range(4):
                cube[(step * 3 + u) * 8 + j] = a[R * u:R * u + R, 128 * j:128 * j + 128]
                cube[(step * 3 + u) * 8 + 4 + j] = b[R * u:R * u + R, 128 * j:128 * j + 128]
        return 0

    lax.fori_loop(0, 13, spread, 0)
    tail = dot(m2l[:, 39 * 384:CLASSES * R], first[0:192, :]).astype(BF16)
    for j in range(4):
        cube[312 + j] = tail[:, 128 * j:128 * j + 128]

    for buffer in (even, odd):
        buffer[...] = jnp.zeros((512, BOX), BF16)

    pair.wait()
    cbuf[chip] = share[...] + share_in[...]

    def far_copies(stage, peers, start, count):
        return [
            pltpu.make_async_remote_copy(
                src_ref=cbuf.at[pl.ds(start, count)],
                dst_ref=cbuf.at[pl.ds(start, count)],
                send_sem=far_send.at[stage, m],
                recv_sem=far_recv.at[stage, m],
                device_id=(peer,),
                device_id_type=MESH,
            )
            for m, peer in enumerate(peers)
        ]

    along_z = far_copies(0, z_peers, chip, 1)
    along_y = far_copies(1, y_peers, (chip // 4) * 4, 4)
    along_x = far_copies(2, x_peers, (chip // 16) * 16, 16)
    for copy in along_z:
        copy.start()

    for distance in DISTANCES:
        @pl.when(valid(distance))
        def _():
            rim_copy(-distance).wait_recv()
    for i in range(BLOCKS):
        g, side = i // 2, i % 2
        columns = jnp.where(lane < 2 * RIM, rims[i].astype(F32), strips[i].astype(F32))
        wide[i] = columns
        table[R * g:R * g + R, 128 * side:128 * side + 128] = columns.astype(BF16)

    index = iota((256, 128), 0).astype(F32).astype(BF16)

    def one_hot(lo, k):
        pieces = []
        for j in range(3):
            wanted = jnp.broadcast_to(lo[k:k + 1, 128 * j:128 * j + 128], (256, 128))
            pieces.append(
                jnp.where(wanted.astype(BF16) == index, jnp.ones((), BF16), jnp.zeros((), BF16))
            )
        return jnp.concatenate(pieces, axis=1)

    def keep(into, p, value):
        for to, start, count in PLACES[p % 5]:
            at = 256 * (p // 5) + to
            into[at:at + count, :] = value[start:start + count]

    def by_lanes(into, p, sought, v):
        wanted = jnp.broadcast_to(sought[:, 128 * v:128 * v + 128], (R, 128))
        inside, tile = wanted & 127, wanted >> 7
        value = jnp.zeros((R, 128), F32)
        for i in range(BLOCKS):
            moved = jnp.take_along_axis(wide[i], inside, axis=1, mode="promise_in_bounds")
            value = jnp.where(tile == i, moved, value)
        value = value.astype(BF16)
        for to, start, count in PLACES[p % 5]:
            at = 256 * (p // 5) + to
            into[at:at + count, 128 * v:128 * v + 128] = value[start:start + count]

    def by_product(step, into, pair_of):
        lo = [lo_ref[pl.ds(step * 10 + p, 1), :] for p in pair_of]
        hi = [hi_ref[pl.ds(step * 10 + p, 1), :] for p in pair_of]
        hot = jnp.concatenate([one_hot(x, 0) for x in lo], axis=1)
        found = dot(table[...], hot)
        for q, p in enumerate(pair_of):
            wanted = jnp.broadcast_to(hi[q], (R, BOX))
            value = jnp.zeros((R, BOX), F32)
            for g in range(GROUPS):
                part_of = found[R * g:R * g + R, BOX * q:BOX * q + BOX]
                value = jnp.where(wanted == g, part_of, value)
            keep(into, p, value.astype(BF16))

    def gather(step, into, other):
        sought = {p: cols_ref[pl.ds(step * 10 + p, 1), :] for p in LANE_SLOTS}
        by_product(step, into, PRODUCT_SLOTS[0])
        by_lanes(into, LANE_SLOTS[0], sought[LANE_SLOTS[0]], 0)
        by_lanes(into, LANE_SLOTS[0], sought[LANE_SLOTS[0]], 1)
        by_product(step, into, PRODUCT_SLOTS[1])
        by_lanes(into, LANE_SLOTS[0], sought[LANE_SLOTS[0]], 2)
        translate(step, other, False)
        by_lanes(into, LANE_SLOTS[1], sought[LANE_SLOTS[1]], 0)
        by_product(step, into, PRODUCT_SLOTS[2])
        by_lanes(into, LANE_SLOTS[1], sought[LANE_SLOTS[1]], 1)
        by_lanes(into, LANE_SLOTS[1], sought[LANE_SLOTS[1]], 2)
        by_product(step, into, PRODUCT_SLOTS[3])

    loads[5].wait()
    acc_a[...] = jnp.zeros(acc_a.shape, F32)
    acc_b[...] = jnp.zeros(acc_b.shape, F32)
    at_lane = iota((R, 128), 1).astype(F32).astype(BF16)
    below_48 = at_lane < jnp.full((), 48, BF16)
    below_96 = at_lane < jnp.full((), 96, BF16)

    def translate(step, source, last):
        first_slot = 10 * jnp.maximum(step - 1, 0)
        lhs = []
        for o in range(8):
            tiles = []
            for chunk in range(2):
                ops = []
                for q in range(5):
                    k = first_slot + 5 * chunk + q
                    if last and chunk and q == 4:
                        k = jnp.minimum(k, K - 1)
                    ops.append(cube[cls[k, o]])
                tiles.append(jnp.where(below_48, ops[0], jnp.where(below_96, ops[1], ops[2])))
                rest = pltpu.roll(ops[2], 32, 1)
                tiles.append(jnp.where(below_48, ops[3], jnp.where(below_96, ops[4], rest)))
            lhs.append(jnp.concatenate(tiles, axis=1))
        acc_a[...] += dot(jnp.concatenate(lhs[0:6], axis=0), source[:, 0:256])
        acc_b[...] += dot(jnp.concatenate(lhs[5:8], axis=0), source[:, 256:384])

    def both(step, _):
        gather(2 * step, even, odd)
        gather(2 * step + 1, odd, even)
        return 0

    lax.fori_loop(0, 3, both, 0)
    for copy in along_z:
        copy.wait()
    for copy in along_y:
        copy.start()
    lax.fori_loop(3, 6, both, 0)
    for copy in along_y:
        copy.wait()
    for copy in along_x:
        copy.start()
    lax.fori_loop(6, STEPS // 2, both, 0)
    for copy in along_x:
        copy.wait()

    for load in loads[6:9]:
        load.wait()
    coarse = cbuf[...].reshape(COARSE, 128)
    mixed_far = dot(coup[...], coarse, HIGHEST)
    mine = jnp.sum(
        jnp.where(iota((COARSE, 128), 0) == chip, mixed_far, 0.0), axis=0, keepdims=True
    )
    far = dot_t(jnp.broadcast_to(mine[:, 0:R], (8, R)), cops[...], HIGHEST)
    tile = (iota((R, BOX), 1) % R == iota((R, BOX), 0)).astype(F32)
    far_tiled = dot(far, tile, HIGHEST)
    terms = l2l[...] * far_tiled[0:1, :]
    by_octant = (iota((BOX, BOX), 0) // R == iota((BOX, BOX), 1) // PARENTS).astype(F32)
    lifted = dot(terms, by_octant, HIGHEST)

    gather(STEPS - 1, even, odd)
    translate(STEPS, even, True)
    left_octant = iota((R, 256), 1) // PARENTS
    right_octant = (iota((R, 128), 1) + 256) // PARENTS
    left, right = acc_a[0:R, :], acc_b[0:R, :]
    for o in range(1, 6):
        left = jnp.where(left_octant == o, acc_a[R * o:R * o + R, :], left)
    for o in (6, 7):
        right = jnp.where(right_octant == o, acc_b[R * (o - 5):R * (o - 5) + R, :], right)
    sums = jnp.concatenate([left, right], axis=1) + lifted
    box = iota((R, BOX), 1)
    out_ref[...] = lanes_from(sums, PARENTS * (box % 8) + box // 8)

    for distance in DISTANCES:
        @pl.when(valid(distance))
        def _():
            rim_copy(distance).wait_send()


def shards(multipoles, partners, partner_offset, classes, m2l_ops, m2m_ops, coarse_ops, coupling, l2l_ops):
    any_space = pl.BlockSpec(memory_space=pl.ANY)
    vmem = pl.BlockSpec(memory_space=pltpu.VMEM)
    dma = pltpu.SemaphoreType.DMA
    return pl.pallas_call(
        kernel,
        name="far_field",
        out_shape=(
            jax.ShapeDtypeStruct((R, BOX), F32),
            jax.ShapeDtypeStruct((R, PARENTS), F32),
        ),
        in_specs=[any_space] * 9,
        out_specs=(vmem, vmem),
        scratch_shapes=[
            pltpu.VMEM((R, BOX), BF16),
            pltpu.VMEM((K, BOX), I32),
            pltpu.VMEM((K, BOX), I32),
            pltpu.SMEM((K, 128), I32),
            pltpu.VMEM((R, CLASSES * R), BF16),
            pltpu.VMEM((R, 8 * R), BF16),
            pltpu.VMEM((R, R), F32),
            pltpu.VMEM((COARSE, COARSE), F32),
            pltpu.VMEM((R, 8 * R), F32),
            pltpu.VMEM((R, 128), BF16),
            pltpu.VMEM((BLOCKS, R, 128), BF16),
            pltpu.VMEM((1, 128), F32),
            pltpu.VMEM((1, 128), F32),
            pltpu.VMEM((COARSE, 1, 128), F32),
            pltpu.VMEM((192, BOX), I32),
            pltpu.VMEM((192, BOX), I32),
            pltpu.VMEM((192, BOX), F32),
            pltpu.VMEM((192, BOX), I32),
            pltpu.VMEM((BLOCKS, R, 128), BF16),
            pltpu.VMEM((GROUPS * R, 256), BF16),
            pltpu.VMEM((BLOCKS, R, 128), F32),
            pltpu.VMEM((CLASSES, R, 128), BF16),
            pltpu.VMEM((512, BOX), BF16),
            pltpu.VMEM((512, BOX), BF16),
            pltpu.VMEM((6 * R, 256), F32),
            pltpu.VMEM((3 * R, 128), F32),
            dma((9,)),
            dma((BLOCKS,)),
            dma((BLOCKS,)),
            dma,
            dma,
            dma((3, 3)),
            dma((3, 3)),
        ],
        compiler_params=pltpu.CompilerParams(
            collective_id=0, has_side_effects=True, vmem_limit_bytes=40 * 1024 * 1024
        ),
    )(*[
        pltpu.with_memory_space_constraint(x, pltpu.HBM)
        for x in (
            multipoles, partners, partner_offset, classes, m2l_ops, m2m_ops, coarse_ops, coupling,
            l2l_ops,
        )
    ])


def solution(mesh):
    placed = (
        P(None, "box"), P(None, "box"), P(None, "box"), P(None, "box"),
        P(), P(), P(), P(), P(),
    )
    return jax.shard_map(
        shards,
        mesh=mesh,
        in_specs=placed,
        out_specs=(P(None, "box"), P(None, "box")),
        check_vma=False,
    )
```

```python
import functools

import jax
import jax.numpy as jnp
from jax import lax
from jax.experimental import pallas as pl
from jax.experimental.pallas import tpu as pltpu
from jax.sharding import PartitionSpec as P

BF16 = jnp.bfloat16
F32 = jnp.float32
I32 = jnp.int32
MESH = pl.DeviceIdType.MESH
HIGHEST = lax.Precision.HIGHEST

DEVICES = 128
R = 48
K = 189
BOX = 384
CLASSES = 316
REACH = 7
RIM = 48
COARSE = 64
PARENTS = BOX // 8
GROUP = 96
BLOCKS = 2 * REACH
GROUPS = BLOCKS // 2
PAD_K = 190
CHUNKS = PAD_K // 5
STEPS = CHUNKS // 2
LANE_SLOTS = (4, 9)
PRODUCT_SLOTS = ((0, 1), (2, 3), (5, 6), (7, 8))
PLACES = (
    ((0, 0, 48),), ((48, 0, 48),), ((96, 0, 32), (240, 32, 16)), ((128, 0, 48),), ((176, 0, 48),),
)


def slot_of(distance):
    return distance + REACH if distance < 0 else distance + REACH - 1


DISTANCES = [s for a in range(1, REACH + 1) for s in (a, -a)]


def dot(a, b, precision=None):
    return jnp.dot(a, b, preferred_element_type=F32, precision=precision)


def dot_t(a, b, precision=None):
    return lax.dot_general(
        a, b, (((1,), (1,)), ((), ())), preferred_element_type=F32, precision=precision
    )


def iota(shape, dim):
    return lax.broadcasted_iota(I32, shape, dim)


def lanes_from(x, source):
    tiles = []
    for v in range(3):
        wanted = source[:, 128 * v:128 * v + 128]
        inside, tile = wanted & 127, wanted >> 7
        found = None
        for u in range(3):
            moved = jnp.take_along_axis(
                x[:, 128 * u:128 * u + 128], inside, axis=1, mode="promise_in_bounds"
            )
            found = moved if u == 0 else jnp.where(tile == u, moved, found)
        tiles.append(found)
    return jnp.concatenate(tiles, axis=1)


def kernel(
    mult_hbm, part_hbm, off_hbm, cls_hbm, m2l_hbm, m2m_hbm, cops_hbm, coup_hbm, l2l_hbm,
    out_ref, par_ref,
    mult, part, off, cls, m2l, m2m, cops, coup, l2l,
    blk, rims, share, share_in, cbuf, cols, cols_ref, lo_ref, hi_ref, strips, table, wide, cube, even, odd, acc_a, acc_b,
    in_sem, rim_send, rim_recv, pair_send, pair_recv, far_send, far_recv,
):
    me = lax.axis_index("box")
    chip = me // 2
    zc, yc, xc = chip % 4, (chip // 4) % 4, chip // 16
    core = me % 2

    loads = [
        pltpu.make_async_copy(src, dst, in_sem.at[i])
        for i, (src, dst) in enumerate(
            [
                (mult_hbm, mult), (m2m_hbm, m2m), (part_hbm, part), (off_hbm, off),
                (m2l_hbm, m2l), (cls_hbm.at[:, pl.ds(0, 128)], cls), (cops_hbm, cops),
                (coup_hbm, coup), (l2l_hbm, l2l),
            ]
        )
    ]
    for load in loads:
        load.start()

    def chip_peer(z, y, x):
        return ((x * 4 + y) * 4 + z) * 2 + core

    z_peers = [chip_peer((zc + m) % 4, yc, xc) for m in (1, 2, 3)]
    y_peers = [chip_peer(zc, (yc + m) % 4, xc) for m in (1, 2, 3)]
    x_peers = [chip_peer(zc, yc, (xc + m) % 4) for m in (1, 2, 3)]
    partner = me + 1 - 2 * core

    def valid(distance):
        return me + distance < DEVICES if distance > 0 else me + distance >= 0

    barrier = pltpu.get_barrier_semaphore()
    for distance in DISTANCES:
        @pl.when(valid(distance))
        def _():
            pl.semaphore_signal(
                barrier, inc=1, device_id=(me + distance,), device_id_type=MESH
            )
    for peer in y_peers + x_peers:
        pl.semaphore_signal(barrier, inc=1, device_id=(peer,), device_id_type=MESH)

    loads[0].wait()
    own = mult[...]
    own32 = own.astype(F32)
    lane = iota((R, 128), 1)
    upper = pltpu.roll(own32[:, 256:384], 96, 1)
    blk[...] = jnp.where(
        lane < RIM, own32[:, 0:128], jnp.where(lane < 2 * RIM, upper, 0.0)
    ).astype(BF16)

    for i in range(BLOCKS):
        if i < BOX // 32:
            piece = own32[:, 128 * (i // 4):128 * (i // 4) + 128]
            shift = (96 - 32 * (i % 4)) % 128
            if shift:
                piece = pltpu.roll(piece, shift, 1)
            strips[i] = jnp.where(lane >= 2 * RIM, piece, 0.0).astype(BF16)
        else:
            strips[i] = jnp.zeros((R, 128), BF16)

    loads[2].wait()
    loads[3].wait()
    within, half = part[...], off[...]
    second = half & 1
    pos = half >> 1
    here = pos == REACH
    local = within + 192 * second
    local_col = ((local >> 5) << 7) + 96 + (local & 31)
    block = jnp.where(pos > REACH, pos - 1, pos)
    remote_col = (block << 7) + within + second * (RIM - 144)
    col = jnp.where(here, local_col, remote_col)
    cols[...] = jnp.zeros((192, BOX), I32)
    cols[0:K, :] = col
    slot = iota((192, BOX), 1)
    col = lanes_from(cols[...], 8 * (slot % PARENTS) + slot // PARENTS)
    cols_ref[...] = col
    lo_ref[...] = (col & 255).astype(F32)
    hi_ref[...] = col >> 8

    expected = jnp.minimum(me, REACH) + jnp.minimum(DEVICES - 1 - me, REACH) + 6
    pl.semaphore_wait(barrier, expected)

    def rim_copy(distance):
        slot = slot_of(-distance)
        return pltpu.make_async_remote_copy(
            src_ref=blk,
            dst_ref=rims.at[slot],
            send_sem=rim_send.at[slot],
            recv_sem=rim_recv.at[slot],
            device_id=(me + distance,),
            device_id_type=MESH,
        )

    for distance in DISTANCES:
        @pl.when(valid(distance))
        def _():
            rim_copy(distance).start()

        @pl.when(jnp.logical_not(valid(distance)))
        def _():
            rims[slot_of(distance)] = jnp.zeros((R, 128), BF16)

    loads[1].wait()
    stacked = jnp.concatenate([m2m[:, R * j:R * j + R] for j in range(8)], axis=0)
    shifted = dot(stacked, own)
    octant = iota((R, BOX), 1) % 8
    mixed = jnp.zeros((R, BOX), F32)
    for j in range(8):
        mixed = jnp.where(octant == j, shifted[R * j:R * j + R], mixed)
    pool = (iota((BOX, PARENTS), 0) // 8 == iota((BOX, PARENTS), 1)).astype(F32)
    parents = dot(mixed, pool, HIGHEST)
    par_ref[...] = parents
    ones = jnp.ones((8, PARENTS), F32)
    total = dot_t(ones, parents, HIGHEST) * jnp.float32(GROUP ** (-0.5))
    share[...] = jnp.zeros((1, 128), F32)
    share[:, 0:R] = total[0:1, :]
    pair = pltpu.make_async_remote_copy(
        src_ref=share, dst_ref=share_in, send_sem=pair_send, recv_sem=pair_recv,
        device_id=(partner,), device_id_type=MESH,
    )
    pair.start()

    loads[4].wait()
    row, column = iota((256, 512), 0), iota((256, 512), 1)
    wanted = R * (column >> 7) + (column & 127) % R
    first = jnp.where(row == wanted, 1.0, 0.0).astype(BF16)
    second_half = jnp.concatenate([jnp.zeros((64, 512), BF16), first[0:192]], axis=0)

    def spread(step, _):
        tops, bottoms = [], []
        for u in range(13):
            base = pl.multiple_of((step * 13 + u) * 384, 128)
            tops.append(m2l[:, pl.ds(base, 256)])
            bottoms.append(m2l[:, pl.ds(pl.multiple_of(base + 128, 128), 256)])
        a = dot(jnp.concatenate(tops, axis=0), first).astype(BF16)
        b = dot(jnp.concatenate(bottoms, axis=0), second_half).astype(BF16)
        for u in range(13):
            for j in range(4):
                cube[(step * 13 + u) * 8 + j] = a[R * u:R * u + R, 128 * j:128 * j + 128]
                cube[(step * 13 + u) * 8 + 4 + j] = b[R * u:R * u + R, 128 * j:128 * j + 128]
        return 0

    lax.fori_loop(0, 3, spread, 0)
    tail = dot(m2l[:, 39 * 384:CLASSES * R], first[0:192, :]).astype(BF16)
    for j in range(4):
        cube[312 + j] = tail[:, 128 * j:128 * j + 128]

    for buffer in (even, odd):
        buffer[...] = jnp.zeros((512, BOX), BF16)

    pair.wait()
    cbuf[chip] = share[...] + share_in[...]

    def far_copies(stage, peers, start, count):
        return [
            pltpu.make_async_remote_copy(
                src_ref=cbuf.at[pl.ds(start, count)],
                dst_ref=cbuf.at[pl.ds(start, count)],
                send_sem=far_send.at[stage, m],
                recv_sem=far_recv.at[stage, m],
                device_id=(peer,),
                device_id_type=MESH,
            )
            for m, peer in enumerate(peers)
        ]

    along_z = far_copies(0, z_peers, chip, 1)
    along_y = far_copies(1, y_peers, (chip // 4) * 4, 4)
    along_x = far_copies(2, x_peers, (chip // 16) * 16, 16)
    for copy in along_z:
        copy.start()

    for distance in DISTANCES:
        @pl.when(valid(distance))
        def _():
            rim_copy(-distance).wait_recv()
    for i in range(BLOCKS):
        g, side = i // 2, i % 2
        columns = jnp.where(lane < 2 * RIM, rims[i].astype(F32), strips[i].astype(F32))
        wide[i] = columns
        table[R * g:R * g + R, 128 * side:128 * side + 128] = columns.astype(BF16)

    index = iota((256, 128), 0).astype(F32).astype(BF16)

    def one_hot(lo, k):
        pieces = []
        for j in range(3):
            wanted = jnp.broadcast_to(lo[k:k + 1, 128 * j:128 * j + 128], (256, 128))
            pieces.append(
                jnp.where(wanted.astype(BF16) == index, jnp.ones((), BF16), jnp.zeros((), BF16))
            )
        return jnp.concatenate(pieces, axis=1)

    def keep(into, p, value):
        for to, start, count in PLACES[p % 5]:
            at = 256 * (p // 5) + to
            into[at:at + count, :] = value[start:start + count]

    def by_lanes(into, p, sought, v):
        wanted = jnp.broadcast_to(sought[:, 128 * v:128 * v + 128], (R, 128))
        inside, tile = wanted & 127, wanted >> 7
        value = None
        for i in range(BLOCKS):
            moved = jnp.take_along_axis(wide[i], inside, axis=1, mode="promise_in_bounds")
            value = moved if i == 0 else jnp.where(tile == i, moved, value)
        value = value.astype(BF16)
        for to, start, count in PLACES[p % 5]:
            at = 256 * (p // 5) + to
            into[at:at + count, 128 * v:128 * v + 128] = value[start:start + count]

    def by_product(step, into, pair_of):
        lo = [lo_ref[pl.ds(step * 10 + p, 1), :] for p in pair_of]
        hi = [hi_ref[pl.ds(step * 10 + p, 1), :] for p in pair_of]
        hot = jnp.concatenate([one_hot(x, 0) for x in lo], axis=1)
        found = dot(table[...], hot)
        for q, p in enumerate(pair_of):
            wanted = jnp.broadcast_to(hi[q], (R, BOX))
            value = found[0:R, BOX * q:BOX * q + BOX]
            for g in range(1, GROUPS):
                part_of = found[R * g:R * g + R, BOX * q:BOX * q + BOX]
                value = jnp.where(wanted == g, part_of, value)
            keep(into, p, value.astype(BF16))

    def gather(step, into, other):
        sought = {p: cols_ref[pl.ds(step * 10 + p, 1), :] for p in LANE_SLOTS}
        by_product(step, into, PRODUCT_SLOTS[0])
        by_lanes(into, LANE_SLOTS[0], sought[LANE_SLOTS[0]], 0)
        by_lanes(into, LANE_SLOTS[0], sought[LANE_SLOTS[0]], 1)
        by_product(step, into, PRODUCT_SLOTS[1])
        by_lanes(into, LANE_SLOTS[0], sought[LANE_SLOTS[0]], 2)
        translate(step, other, False)
        by_lanes(into, LANE_SLOTS[1], sought[LANE_SLOTS[1]], 0)
        by_product(step, into, PRODUCT_SLOTS[2])
        by_lanes(into, LANE_SLOTS[1], sought[LANE_SLOTS[1]], 1)
        by_lanes(into, LANE_SLOTS[1], sought[LANE_SLOTS[1]], 2)
        by_product(step, into, PRODUCT_SLOTS[3])

    loads[5].wait()
    acc_a[...] = jnp.zeros(acc_a.shape, F32)
    acc_b[...] = jnp.zeros(acc_b.shape, F32)
    at_lane = iota((R, 128), 1).astype(F32).astype(BF16)
    below_48 = at_lane < jnp.full((), 48, BF16)
    below_96 = at_lane < jnp.full((), 96, BF16)

    def translate(step, source, last):
        first_slot = 10 * jnp.maximum(step - 1, 0)
        lhs = []
        for o in range(8):
            tiles = []
            for chunk in range(2):
                ops = []
                for q in range(5):
                    k = first_slot + 5 * chunk + q
                    if last and chunk and q == 4:
                        ops.append(jnp.zeros((R, 128), BF16))
                    else:
                        ops.append(cube[cls[k, o]])
                tiles.append(jnp.where(below_48, ops[0], jnp.where(below_96, ops[1], ops[2])))
                rest = pltpu.roll(ops[2], 32, 1)
                tiles.append(jnp.where(below_48, ops[3], jnp.where(below_96, ops[4], rest)))
            lhs.append(jnp.concatenate(tiles, axis=1))
        acc_a[...] += dot(jnp.concatenate(lhs[0:6], axis=0), source[:, 0:256])
        acc_b[...] += dot(jnp.concatenate(lhs[5:8], axis=0), source[:, 256:384])

    def several(step, _):
        @pl.when(step == 1)
        def _():
            for copy in along_z:
                copy.wait()
            for copy in along_y:
                copy.start()

        @pl.when(step == 2)
        def _():
            for copy in along_y:
                copy.wait()
            for copy in along_x:
                copy.start()

        gather(6 * step + 0, even, odd)
        gather(6 * step + 1, odd, even)
        gather(6 * step + 2, even, odd)
        gather(6 * step + 3, odd, even)
        gather(6 * step + 4, even, odd)
        gather(6 * step + 5, odd, even)
        return 0

    lax.fori_loop(0, 3, several, 0)
    for copy in along_x:
        copy.wait()

    for load in loads[6:9]:
        load.wait()
    coarse = cbuf[...].reshape(COARSE, 128)
    mixed_far = dot(coup[...], coarse, HIGHEST)
    mine = jnp.sum(
        jnp.where(iota((COARSE, 128), 0) == chip, mixed_far, 0.0), axis=0, keepdims=True
    )
    far = dot_t(jnp.broadcast_to(mine[:, 0:R], (8, R)), cops[...], HIGHEST)
    tile = (iota((R, BOX), 1) % R == iota((R, BOX), 0)).astype(F32)
    far_tiled = dot(far, tile, HIGHEST)
    terms = l2l[...] * far_tiled[0:1, :]
    by_octant = (iota((BOX, BOX), 0) // R == iota((BOX, BOX), 1) // PARENTS).astype(F32)
    lifted = dot(terms, by_octant, HIGHEST)

    gather(STEPS - 1, even, odd)
    translate(STEPS, even, True)
    left_octant = iota((R, 256), 1) // PARENTS
    right_octant = (iota((R, 128), 1) + 256) // PARENTS
    left, right = acc_a[0:R, :], acc_b[0:R, :]
    for o in range(1, 6):
        left = jnp.where(left_octant == o, acc_a[R * o:R * o + R, :], left)
    for o in (6, 7):
        right = jnp.where(right_octant == o, acc_b[R * (o - 5):R * (o - 5) + R, :], right)
    sums = jnp.concatenate([left, right], axis=1) + lifted
    box = iota((R, BOX), 1)
    out_ref[...] = lanes_from(sums, PARENTS * (box % 8) + box // 8)

    for distance in DISTANCES:
        @pl.when(valid(distance))
        def _():
            rim_copy(distance).wait_send()


def shards(multipoles, partners, partner_offset, classes, m2l_ops, m2m_ops, coarse_ops, coupling, l2l_ops):
    any_space = pl.BlockSpec(memory_space=pl.ANY)
    vmem = pl.BlockSpec(memory_space=pltpu.VMEM)
    dma = pltpu.SemaphoreType.DMA
    return pl.pallas_call(
        kernel,
        name="far_field",
        out_shape=(
            jax.ShapeDtypeStruct((R, BOX), F32),
            jax.ShapeDtypeStruct((R, PARENTS), F32),
        ),
        in_specs=[any_space] * 9,
        out_specs=(vmem, vmem),
        scratch_shapes=[
            pltpu.VMEM((R, BOX), BF16),
            pltpu.VMEM((K, BOX), I32),
            pltpu.VMEM((K, BOX), I32),
            pltpu.SMEM((K, 128), I32),
            pltpu.VMEM((R, CLASSES * R), BF16),
            pltpu.VMEM((R, 8 * R), BF16),
            pltpu.VMEM((R, R), F32),
            pltpu.VMEM((COARSE, COARSE), F32),
            pltpu.VMEM((R, 8 * R), F32),
            pltpu.VMEM((R, 128), BF16),
            pltpu.VMEM((BLOCKS, R, 128), BF16),
            pltpu.VMEM((1, 128), F32),
            pltpu.VMEM((1, 128), F32),
            pltpu.VMEM((COARSE, 1, 128), F32),
            pltpu.VMEM((192, BOX), I32),
            pltpu.VMEM((192, BOX), I32),
            pltpu.VMEM((192, BOX), F32),
            pltpu.VMEM((192, BOX), I32),
            pltpu.VMEM((BLOCKS, R, 128), BF16),
            pltpu.VMEM((GROUPS * R, 256), BF16),
            pltpu.VMEM((BLOCKS, R, 128), F32),
            pltpu.VMEM((CLASSES, R, 128), BF16),
            pltpu.VMEM((512, BOX), BF16),
            pltpu.VMEM((512, BOX), BF16),
            pltpu.VMEM((6 * R, 256), F32),
            pltpu.VMEM((3 * R, 128), F32),
            dma((9,)),
            dma((BLOCKS,)),
            dma((BLOCKS,)),
            dma,
            dma,
            dma((3, 3)),
            dma((3, 3)),
        ],
        compiler_params=pltpu.CompilerParams(
            collective_id=0, has_side_effects=True, vmem_limit_bytes=40 * 1024 * 1024
        ),
    )(*[
        pltpu.with_memory_space_constraint(x, pltpu.HBM)
        for x in (
            multipoles, partners, partner_offset, classes, m2l_ops, m2m_ops, coarse_ops, coupling,
            l2l_ops,
        )
    ])


def solution(mesh):
    placed = (
        P(None, "box"), P(None, "box"), P(None, "box"), P(None, "box"),
        P(), P(), P(), P(), P(),
    )
    return jax.shard_map(
        shards,
        mesh=mesh,
        in_specs=placed,
        out_specs=(P(None, "box"), P(None, "box")),
        check_vma=False,
    )
```

```python
import functools

import jax
import jax.numpy as jnp
from jax import lax
from jax.experimental import pallas as pl
from jax.experimental.pallas import tpu as pltpu
from jax.sharding import PartitionSpec as P

BF16 = jnp.bfloat16
F32 = jnp.float32
I32 = jnp.int32
MESH = pl.DeviceIdType.MESH
HIGHEST = lax.Precision.HIGHEST

DEVICES = 128
R = 48
K = 189
BOX = 384
CLASSES = 316
REACH = 7
RIM = 48
COARSE = 64
PARENTS = BOX // 8
GROUP = 96
BLOCKS = 2 * REACH
GROUPS = BLOCKS // 2
PAD_K = 190
CHUNKS = PAD_K // 5
STEPS = CHUNKS // 2
LANE_SLOTS = (4, 9)
PRODUCT_SLOTS = ((0, 1), (2, 3), (5, 6), (7, 8))
PLACES = (
    ((0, 0, 48),), ((48, 0, 48),), ((96, 0, 32), (240, 32, 16)), ((128, 0, 48),), ((176, 0, 48),),
)


def slot_of(distance):
    return distance + REACH if distance < 0 else distance + REACH - 1


DISTANCES = [s for a in range(1, REACH + 1) for s in (a, -a)]


def dot(a, b, precision=None):
    return jnp.dot(a, b, preferred_element_type=F32, precision=precision)


def dot_t(a, b, precision=None):
    return lax.dot_general(
        a, b, (((1,), (1,)), ((), ())), preferred_element_type=F32, precision=precision
    )


def iota(shape, dim):
    return lax.broadcasted_iota(I32, shape, dim)


def lanes_from(x, source):
    tiles = []
    for v in range(3):
        wanted = source[:, 128 * v:128 * v + 128]
        inside, tile = wanted & 127, wanted >> 7
        found = None
        for u in range(3):
            moved = jnp.take_along_axis(
                x[:, 128 * u:128 * u + 128], inside, axis=1, mode="promise_in_bounds"
            )
            found = moved if u == 0 else jnp.where(tile == u, moved, found)
        tiles.append(found)
    return jnp.concatenate(tiles, axis=1)


def kernel(
    mult_hbm, part_hbm, off_hbm, cls_hbm, m2l_hbm, m2m_hbm, cops_hbm, coup_hbm, l2l_hbm,
    out_ref, par_ref,
    mult, part, off, cls, m2l, m2m, cops, coup, l2l,
    blk, rims, share, share_in, cbuf, cols, cols_ref, lo_ref, hi_ref, strips, table, wide, cube, even, odd, acc_a, acc_b,
    in_sem, rim_send, rim_recv, pair_send, pair_recv, far_send, far_recv,
):
    me = lax.axis_index("box")
    chip = me // 2
    zc, yc, xc = chip % 4, (chip // 4) % 4, chip // 16
    core = me % 2

    loads = [
        pltpu.make_async_copy(src, dst, in_sem.at[i])
        for i, (src, dst) in enumerate(
            [
                (mult_hbm, mult), (m2m_hbm, m2m), (part_hbm, part), (off_hbm, off),
                (m2l_hbm, m2l), (cls_hbm.at[:, pl.ds(0, 128)], cls), (cops_hbm, cops),
                (coup_hbm, coup), (l2l_hbm, l2l),
            ]
        )
    ]
    for load in loads:
        load.start()

    def chip_peer(z, y, x):
        return ((x * 4 + y) * 4 + z) * 2 + core

    z_peers = [chip_peer((zc + m) % 4, yc, xc) for m in (1, 2, 3)]
    y_peers = [chip_peer(zc, (yc + m) % 4, xc) for m in (1, 2, 3)]
    x_peers = [chip_peer(zc, yc, (xc + m) % 4) for m in (1, 2, 3)]
    partner = me + 1 - 2 * core

    def valid(distance):
        return me + distance < DEVICES if distance > 0 else me + distance >= 0

    barrier = pltpu.get_barrier_semaphore()
    for distance in DISTANCES:
        @pl.when(valid(distance))
        def _():
            pl.semaphore_signal(
                barrier, inc=1, device_id=(me + distance,), device_id_type=MESH
            )
    for peer in y_peers + x_peers:
        pl.semaphore_signal(barrier, inc=1, device_id=(peer,), device_id_type=MESH)

    loads[0].wait()
    own = mult[...]
    own32 = own.astype(F32)
    lane = iota((R, 128), 1)
    upper = pltpu.roll(own32[:, 256:384], 96, 1)
    blk[...] = jnp.where(
        lane < RIM, own32[:, 0:128], jnp.where(lane < 2 * RIM, upper, 0.0)
    ).astype(BF16)

    for i in range(BLOCKS):
        if i < BOX // 32:
            piece = own32[:, 128 * (i // 4):128 * (i // 4) + 128]
            shift = (96 - 32 * (i % 4)) % 128
            if shift:
                piece = pltpu.roll(piece, shift, 1)
            strips[i] = jnp.where(lane >= 2 * RIM, piece, 0.0).astype(BF16)
        else:
            strips[i] = jnp.zeros((R, 128), BF16)

    loads[2].wait()
    loads[3].wait()
    within, half = part[...], off[...]
    second = half & 1
    pos = half >> 1
    here = pos == REACH
    local = within + 192 * second
    local_col = ((local >> 5) << 7) + 96 + (local & 31)
    block = jnp.where(pos > REACH, pos - 1, pos)
    remote_col = (block << 7) + within + second * (RIM - 144)
    col = jnp.where(here, local_col, remote_col)
    cols[...] = jnp.zeros((192, BOX), I32)
    cols[0:K, :] = col
    slot = iota((192, BOX), 1)
    col = lanes_from(cols[...], 8 * (slot % PARENTS) + slot // PARENTS)
    cols_ref[...] = col
    lo_ref[...] = (col & 255).astype(F32)
    hi_ref[...] = col >> 8

    expected = jnp.minimum(me, REACH) + jnp.minimum(DEVICES - 1 - me, REACH) + 6
    pl.semaphore_wait(barrier, expected)

    def rim_copy(distance):
        slot = slot_of(-distance)
        return pltpu.make_async_remote_copy(
            src_ref=blk,
            dst_ref=rims.at[slot],
            send_sem=rim_send.at[slot],
            recv_sem=rim_recv.at[slot],
            device_id=(me + distance,),
            device_id_type=MESH,
        )

    for distance in DISTANCES:
        @pl.when(valid(distance))
        def _():
            rim_copy(distance).start()

        @pl.when(jnp.logical_not(valid(distance)))
        def _():
            rims[slot_of(distance)] = jnp.zeros((R, 128), BF16)

    loads[1].wait()
    stacked = jnp.concatenate([m2m[:, R * j:R * j + R] for j in range(8)], axis=0)
    shifted = dot(stacked, own)
    octant = iota((R, BOX), 1) % 8
    mixed = jnp.zeros((R, BOX), F32)
    for j in range(8):
        mixed = jnp.where(octant == j, shifted[R * j:R * j + R], mixed)
    pool = (iota((BOX, PARENTS), 0) // 8 == iota((BOX, PARENTS), 1)).astype(F32)
    parents = dot(mixed, pool, HIGHEST)
    par_ref[...] = parents
    ones = jnp.ones((8, PARENTS), F32)
    total = dot_t(ones, parents, HIGHEST) * jnp.float32(GROUP ** (-0.5))
    share[...] = jnp.zeros((1, 128), F32)
    share[:, 0:R] = total[0:1, :]
    pair = pltpu.make_async_remote_copy(
        src_ref=share, dst_ref=share_in, send_sem=pair_send, recv_sem=pair_recv,
        device_id=(partner,), device_id_type=MESH,
    )
    pair.start()

    loads[4].wait()
    row, column = iota((256, 512), 0), iota((256, 512), 1)
    wanted = R * (column >> 7) + (column & 127) % R
    first = jnp.where(row == wanted, 1.0, 0.0).astype(BF16)
    second_half = jnp.concatenate([jnp.zeros((64, 512), BF16), first[0:192]], axis=0)

    def spread(step, _):
        tops, bottoms = [], []
        for u in range(13):
            base = pl.multiple_of((step * 13 + u) * 384, 128)
            tops.append(m2l[:, pl.ds(base, 256)])
            bottoms.append(m2l[:, pl.ds(pl.multiple_of(base + 128, 128), 256)])
        a = dot(jnp.concatenate(tops, axis=0), first).astype(BF16)
        b = dot(jnp.concatenate(bottoms, axis=0), second_half).astype(BF16)
        for u in range(13):
            for j in range(4):
                cube[(step * 13 + u) * 8 + j] = a[R * u:R * u + R, 128 * j:128 * j + 128]
                cube[(step * 13 + u) * 8 + 4 + j] = b[R * u:R * u + R, 128 * j:128 * j + 128]
        return 0

    lax.fori_loop(0, 3, spread, 0)
    tail = dot(m2l[:, 39 * 384:CLASSES * R], first[0:192, :]).astype(BF16)
    for j in range(4):
        cube[312 + j] = tail[:, 128 * j:128 * j + 128]

    for buffer in (even, odd):
        buffer[...] = jnp.zeros((512, BOX), BF16)

    pair.wait()
    cbuf[chip] = share[...] + share_in[...]

    def far_copies(stage, peers, start, count):
        return [
            pltpu.make_async_remote_copy(
                src_ref=cbuf.at[pl.ds(start, count)],
                dst_ref=cbuf.at[pl.ds(start, count)],
                send_sem=far_send.at[stage, m],
                recv_sem=far_recv.at[stage, m],
                device_id=(peer,),
                device_id_type=MESH,
            )
            for m, peer in enumerate(peers)
        ]

    along_z = far_copies(0, z_peers, chip, 1)
    along_y = far_copies(1, y_peers, (chip // 4) * 4, 4)
    along_x = far_copies(2, x_peers, (chip // 16) * 16, 16)
    for copy in along_z:
        copy.start()

    for distance in DISTANCES:
        @pl.when(valid(distance))
        def _():
            rim_copy(-distance).wait_recv()
    for i in range(BLOCKS):
        g, side = i // 2, i % 2
        columns = jnp.where(lane < 2 * RIM, rims[i].astype(F32), strips[i].astype(F32))
        wide[i] = columns
        table[R * g:R * g + R, 128 * side:128 * side + 128] = columns.astype(BF16)

    index = iota((256, 128), 0).astype(F32).astype(BF16)

    def one_hot(lo, k):
        pieces = []
        for j in range(3):
            wanted = jnp.broadcast_to(lo[k:k + 1, 128 * j:128 * j + 128], (256, 128))
            pieces.append(
                jnp.where(wanted.astype(BF16) == index, jnp.ones((), BF16), jnp.zeros((), BF16))
            )
        return jnp.concatenate(pieces, axis=1)

    def keep(into, p, value):
        for to, start, count in PLACES[p % 5]:
            at = 256 * (p // 5) + to
            into[at:at + count, :] = value[start:start + count]

    def by_lanes(into, p, sought, v):
        wanted = jnp.broadcast_to(sought[:, 128 * v:128 * v + 128], (R, 128))
        inside, tile = wanted & 127, wanted >> 7
        value = None
        for i in range(BLOCKS):
            moved = jnp.take_along_axis(wide[i], inside, axis=1, mode="promise_in_bounds")
            value = moved if i == 0 else jnp.where(tile == i, moved, value)
        value = value.astype(BF16)
        for to, start, count in PLACES[p % 5]:
            at = 256 * (p // 5) + to
            into[at:at + count, 128 * v:128 * v + 128] = value[start:start + count]

    def by_product(step, into, pair_of):
        lo = [lo_ref[pl.ds(step * 10 + p, 1), :] for p in pair_of]
        hi = [hi_ref[pl.ds(step * 10 + p, 1), :] for p in pair_of]
        hot = jnp.concatenate([one_hot(x, 0) for x in lo], axis=1)
        found = dot(table[...], hot)
        for q, p in enumerate(pair_of):
            wanted = jnp.broadcast_to(hi[q], (R, BOX))
            value = found[0:R, BOX * q:BOX * q + BOX]
            for g in range(1, GROUPS):
                part_of = found[R * g:R * g + R, BOX * q:BOX * q + BOX]
                value = jnp.where(wanted == g, part_of, value)
            keep(into, p, value.astype(BF16))

    def gather(step, into, other):
        sought = {p: cols_ref[pl.ds(step * 10 + p, 1), :] for p in LANE_SLOTS}
        by_product(step, into, PRODUCT_SLOTS[0])
        by_lanes(into, LANE_SLOTS[0], sought[LANE_SLOTS[0]], 0)
        by_lanes(into, LANE_SLOTS[0], sought[LANE_SLOTS[0]], 1)
        by_product(step, into, PRODUCT_SLOTS[1])
        by_lanes(into, LANE_SLOTS[0], sought[LANE_SLOTS[0]], 2)
        translate(step, other, False)
        by_lanes(into, LANE_SLOTS[1], sought[LANE_SLOTS[1]], 0)
        by_product(step, into, PRODUCT_SLOTS[2])
        by_lanes(into, LANE_SLOTS[1], sought[LANE_SLOTS[1]], 1)
        by_lanes(into, LANE_SLOTS[1], sought[LANE_SLOTS[1]], 2)
        by_product(step, into, PRODUCT_SLOTS[3])

    loads[5].wait()
    acc_a[...] = jnp.zeros(acc_a.shape, F32)
    acc_b[...] = jnp.zeros(acc_b.shape, F32)
    at_lane = iota((R, 128), 1).astype(F32).astype(BF16)
    below_48 = at_lane < jnp.full((), 48, BF16)
    below_96 = at_lane < jnp.full((), 96, BF16)

    def translate(step, source, last):
        first_slot = 10 * jnp.maximum(step - 1, 0)
        lhs = []
        for o in range(8):
            tiles = []
            for chunk in range(2):
                ops = []
                for q in range(5):
                    k = first_slot + 5 * chunk + q
                    if last and chunk and q == 4:
                        ops.append(jnp.zeros((R, 128), BF16))
                    else:
                        ops.append(cube[cls[k, o]])
                tiles.append(jnp.where(below_48, ops[0], jnp.where(below_96, ops[1], ops[2])))
                rest = pltpu.roll(ops[2], 32, 1)
                tiles.append(jnp.where(below_48, ops[3], jnp.where(below_96, ops[4], rest)))
            lhs.append(jnp.concatenate(tiles, axis=1))
        acc_a[...] += dot(jnp.concatenate(lhs[0:5], axis=0), source[:, 0:256])
        acc_b[...] += dot(jnp.concatenate(lhs[5:8], axis=0), source[:, 128:384])

    def several(step, _):
        @pl.when(step == 1)
        def _():
            for distance in DISTANCES:
                @pl.when(valid(distance))
                def _():
                    rim_copy(distance).wait_send()
            for copy in along_z:
                copy.wait()
            for copy in along_y:
                copy.start()

        @pl.when(step == 2)
        def _():
            for copy in along_y:
                copy.wait()
            for copy in along_x:
                copy.start()

        gather(6 * step + 0, even, odd)
        gather(6 * step + 1, odd, even)
        gather(6 * step + 2, even, odd)
        gather(6 * step + 3, odd, even)
        gather(6 * step + 4, even, odd)
        gather(6 * step + 5, odd, even)
        return 0

    lax.fori_loop(0, 3, several, 0)
    for copy in along_x:
        copy.wait()

    for load in loads[6:9]:
        load.wait()
    coarse = cbuf[...].reshape(COARSE, 128)
    mixed_far = dot(coup[...], coarse, HIGHEST)
    mine = jnp.sum(
        jnp.where(iota((COARSE, 128), 0) == chip, mixed_far, 0.0), axis=0, keepdims=True
    )
    far = dot_t(jnp.broadcast_to(mine[:, 0:R], (8, R)), cops[...], HIGHEST)
    tile = (iota((R, BOX), 1) % R == iota((R, BOX), 0)).astype(F32)
    far_tiled = dot(far, tile, HIGHEST)
    terms = l2l[...] * far_tiled[0:1, :]
    by_octant = (iota((BOX, BOX), 0) // R == iota((BOX, BOX), 1) // PARENTS).astype(F32)
    lifted = dot(terms, by_octant, HIGHEST)

    gather(STEPS - 1, even, odd)
    translate(STEPS, even, True)
    octant = iota((R, BOX), 1) // PARENTS
    none = jnp.zeros((R, 128), F32)
    sums = jnp.concatenate([acc_a[0:R, :], none], axis=1)
    for o in range(1, 8):
        if o < 5:
            rows = jnp.concatenate([acc_a[R * o:R * o + R, :], none], axis=1)
        else:
            rows = jnp.concatenate([none, acc_b[R * (o - 5):R * (o - 5) + R, :]], axis=1)
        sums = jnp.where(octant == o, rows, sums)
    sums = sums + lifted
    box = iota((R, BOX), 1)
    out_ref[...] = lanes_from(sums, PARENTS * (box % 8) + box // 8)


def shards(multipoles, partners, partner_offset, classes, m2l_ops, m2m_ops, coarse_ops, coupling, l2l_ops):
    any_space = pl.BlockSpec(memory_space=pl.ANY)
    vmem = pl.BlockSpec(memory_space=pltpu.VMEM)
    dma = pltpu.SemaphoreType.DMA
    return pl.pallas_call(
        kernel,
        name="far_field",
        out_shape=(
            jax.ShapeDtypeStruct((R, BOX), F32),
            jax.ShapeDtypeStruct((R, PARENTS), F32),
        ),
        in_specs=[any_space] * 9,
        out_specs=(vmem, vmem),
        scratch_shapes=[
            pltpu.VMEM((R, BOX), BF16),
            pltpu.VMEM((K, BOX), I32),
            pltpu.VMEM((K, BOX), I32),
            pltpu.SMEM((K, 128), I32),
            pltpu.VMEM((R, CLASSES * R), BF16),
            pltpu.VMEM((R, 8 * R), BF16),
            pltpu.VMEM((R, R), F32),
            pltpu.VMEM((COARSE, COARSE), F32),
            pltpu.VMEM((R, 8 * R), F32),
            pltpu.VMEM((R, 128), BF16),
            pltpu.VMEM((BLOCKS, R, 128), BF16),
            pltpu.VMEM((1, 128), F32),
            pltpu.VMEM((1, 128), F32),
            pltpu.VMEM((COARSE, 1, 128), F32),
            pltpu.VMEM((192, BOX), I32),
            pltpu.VMEM((192, BOX), I32),
            pltpu.VMEM((192, BOX), F32),
            pltpu.VMEM((192, BOX), I32),
            pltpu.VMEM((BLOCKS, R, 128), BF16),
            pltpu.VMEM((GROUPS * R, 256), BF16),
            pltpu.VMEM((BLOCKS, R, 128), F32),
            pltpu.VMEM((CLASSES, R, 128), BF16),
            pltpu.VMEM((512, BOX), BF16),
            pltpu.VMEM((512, BOX), BF16),
            pltpu.VMEM((5 * R, 256), F32),
            pltpu.VMEM((3 * R, 256), F32),
            dma((9,)),
            dma((BLOCKS,)),
            dma((BLOCKS,)),
            dma,
            dma,
            dma((3, 3)),
            dma((3, 3)),
        ],
        compiler_params=pltpu.CompilerParams(
            collective_id=0, has_side_effects=True, vmem_limit_bytes=40 * 1024 * 1024
        ),
    )(*[
        pltpu.with_memory_space_constraint(x, pltpu.HBM)
        for x in (
            multipoles, partners, partner_offset, classes, m2l_ops, m2m_ops, coarse_ops, coupling,
            l2l_ops,
        )
    ])


def solution(mesh):
    placed = (
        P(None, "box"), P(None, "box"), P(None, "box"), P(None, "box"),
        P(), P(), P(), P(), P(),
    )
    return jax.shard_map(
        shards,
        mesh=mesh,
        in_specs=placed,
        out_specs=(P(None, "box"), P(None, "box")),
        check_vma=False,
    )
```

```python
import functools

import jax
import jax.numpy as jnp
from jax import lax
from jax.experimental import pallas as pl
from jax.experimental.pallas import tpu as pltpu
from jax.sharding import PartitionSpec as P

BF16 = jnp.bfloat16
F32 = jnp.float32
I32 = jnp.int32
MESH = pl.DeviceIdType.MESH
HIGHEST = lax.Precision.HIGHEST

DEVICES = 128
R = 48
K = 189
BOX = 384
CLASSES = 316
REACH = 7
RIM = 48
COARSE = 64
PARENTS = BOX // 8
GROUP = 96
BLOCKS = 2 * REACH
GROUPS = BLOCKS // 2
PAD_K = 190
CHUNKS = PAD_K // 5
STEPS = CHUNKS // 2
LANE_SLOTS = (4, 9)
PRODUCT_SLOTS = ((0, 1), (2, 3), (5, 6), (7, 8))
PLACES = (
    ((0, 0, 48),), ((48, 0, 48),), ((96, 0, 32), (240, 32, 16)), ((128, 0, 48),), ((176, 0, 48),),
)


def slot_of(distance):
    return distance + REACH if distance < 0 else distance + REACH - 1


DISTANCES = [s for a in range(1, REACH + 1) for s in (a, -a)]


def dot(a, b, precision=None):
    return jnp.dot(a, b, preferred_element_type=F32, precision=precision)


def dot_t(a, b, precision=None):
    return lax.dot_general(
        a, b, (((1,), (1,)), ((), ())), preferred_element_type=F32, precision=precision
    )


def iota(shape, dim):
    return lax.broadcasted_iota(I32, shape, dim)


def lanes_from(x, source):
    tiles = []
    for v in range(3):
        wanted = source[:, 128 * v:128 * v + 128]
        inside, tile = wanted & 127, wanted >> 7
        found = None
        for u in range(3):
            moved = jnp.take_along_axis(
                x[:, 128 * u:128 * u + 128], inside, axis=1, mode="promise_in_bounds"
            )
            found = moved if u == 0 else jnp.where(tile == u, moved, found)
        tiles.append(found)
    return jnp.concatenate(tiles, axis=1)


def kernel(
    mult_hbm, part_hbm, off_hbm, cls_hbm, m2l_hbm, m2m_hbm, cops_hbm, coup_hbm, l2l_hbm,
    out_ref, par_ref,
    mult, part, off, cls, m2l, m2m, cops, coup, l2l,
    blk, rims, share, share_in, cbuf, cols, cols_ref, lo_ref, hi_ref, strips, table, wide, cube, even, odd, acc_a, acc_b,
    in_sem, rim_send, rim_recv, pair_send, pair_recv, far_send, far_recv,
):
    me = lax.axis_index("box")
    chip = me // 2
    zc, yc, xc = chip % 4, (chip // 4) % 4, chip // 16
    core = me % 2

    loads = [
        pltpu.make_async_copy(src, dst, in_sem.at[i])
        for i, (src, dst) in enumerate(
            [
                (mult_hbm, mult), (m2m_hbm, m2m), (part_hbm, part), (off_hbm, off),
                (m2l_hbm, m2l), (cls_hbm.at[:, pl.ds(0, 128)], cls), (cops_hbm, cops),
                (coup_hbm, coup), (l2l_hbm, l2l),
            ]
        )
    ]
    for load in loads:
        load.start()

    def chip_peer(z, y, x):
        return ((x * 4 + y) * 4 + z) * 2 + core

    z_peers = [chip_peer((zc + m) % 4, yc, xc) for m in (1, 2, 3)]
    y_peers = [chip_peer(zc, (yc + m) % 4, xc) for m in (1, 2, 3)]
    x_peers = [chip_peer(zc, yc, (xc + m) % 4) for m in (1, 2, 3)]
    partner = me + 1 - 2 * core

    def valid(distance):
        return me + distance < DEVICES if distance > 0 else me + distance >= 0

    barrier = pltpu.get_barrier_semaphore()
    for distance in DISTANCES:
        @pl.when(valid(distance))
        def _():
            pl.semaphore_signal(
                barrier, inc=1, device_id=(me + distance,), device_id_type=MESH
            )
    for peer in y_peers + x_peers:
        pl.semaphore_signal(barrier, inc=1, device_id=(peer,), device_id_type=MESH)

    loads[0].wait()
    own = mult[...]
    own32 = own.astype(F32)
    lane = iota((R, 128), 1)
    upper = pltpu.roll(own32[:, 256:384], 96, 1)
    blk[...] = jnp.where(
        lane < RIM, own32[:, 0:128], jnp.where(lane < 2 * RIM, upper, 0.0)
    ).astype(BF16)

    for i in range(BLOCKS):
        if i < BOX // 32:
            piece = own32[:, 128 * (i // 4):128 * (i // 4) + 128]
            shift = (96 - 32 * (i % 4)) % 128
            if shift:
                piece = pltpu.roll(piece, shift, 1)
            strips[i] = jnp.where(lane >= 2 * RIM, piece, 0.0).astype(BF16)
        else:
            strips[i] = jnp.zeros((R, 128), BF16)

    loads[2].wait()
    loads[3].wait()
    within, half = part[...], off[...]
    second = half & 1
    pos = half >> 1
    here = pos == REACH
    local = within + 192 * second
    local_col = ((local >> 5) << 7) + 96 + (local & 31)
    block = jnp.where(pos > REACH, pos - 1, pos)
    remote_col = (block << 7) + within + second * (RIM - 144)
    col = jnp.where(here, local_col, remote_col)
    cols[...] = jnp.zeros((192, BOX), I32)
    cols[0:K, :] = col
    slot = iota((192, BOX), 1)
    col = lanes_from(cols[...], 8 * (slot % PARENTS) + slot // PARENTS)
    cols_ref[...] = col
    lo_ref[...] = (col & 255).astype(F32)
    hi_ref[...] = col >> 8

    expected = jnp.minimum(me, REACH) + jnp.minimum(DEVICES - 1 - me, REACH) + 6
    pl.semaphore_wait(barrier, expected)

    def rim_copy(distance):
        slot = slot_of(-distance)
        return pltpu.make_async_remote_copy(
            src_ref=blk,
            dst_ref=rims.at[slot],
            send_sem=rim_send.at[slot],
            recv_sem=rim_recv.at[slot],
            device_id=(me + distance,),
            device_id_type=MESH,
        )

    for distance in DISTANCES:
        @pl.when(valid(distance))
        def _():
            rim_copy(distance).start()

        @pl.when(jnp.logical_not(valid(distance)))
        def _():
            rims[slot_of(distance)] = jnp.zeros((R, 128), BF16)

    loads[1].wait()
    stacked = jnp.concatenate([m2m[:, R * j:R * j + R] for j in range(8)], axis=0)
    shifted = dot(stacked, own)
    octant = iota((R, BOX), 1) % 8
    mixed = jnp.zeros((R, BOX), F32)
    for j in range(8):
        mixed = jnp.where(octant == j, shifted[R * j:R * j + R], mixed)
    pool = (iota((BOX, PARENTS), 0) // 8 == iota((BOX, PARENTS), 1)).astype(F32)
    parents = dot(mixed, pool, HIGHEST)
    par_ref[...] = parents
    ones = jnp.ones((8, PARENTS), F32)
    total = dot_t(ones, parents, HIGHEST) * jnp.float32(GROUP ** (-0.5))
    share[...] = jnp.zeros((1, 128), F32)
    share[:, 0:R] = total[0:1, :]
    pair = pltpu.make_async_remote_copy(
        src_ref=share, dst_ref=share_in, send_sem=pair_send, recv_sem=pair_recv,
        device_id=(partner,), device_id_type=MESH,
    )
    pair.start()

    loads[4].wait()
    row, column = iota((256, 512), 0), iota((256, 512), 1)
    wanted = R * (column >> 7) + (column & 127) % R
    first = jnp.where(row == wanted, 1.0, 0.0).astype(BF16)
    second_half = jnp.concatenate([jnp.zeros((64, 512), BF16), first[0:192]], axis=0)

    def spread(step, _):
        tops, bottoms = [], []
        for u in range(13):
            base = pl.multiple_of((step * 13 + u) * 384, 128)
            tops.append(m2l[:, pl.ds(base, 256)])
            bottoms.append(m2l[:, pl.ds(pl.multiple_of(base + 128, 128), 256)])
        a = dot(jnp.concatenate(tops, axis=0), first).astype(BF16)
        b = dot(jnp.concatenate(bottoms, axis=0), second_half).astype(BF16)
        for u in range(13):
            for j in range(4):
                cube[(step * 13 + u) * 8 + j] = a[R * u:R * u + R, 128 * j:128 * j + 128]
                cube[(step * 13 + u) * 8 + 4 + j] = b[R * u:R * u + R, 128 * j:128 * j + 128]
        return 0

    lax.fori_loop(0, 3, spread, 0)
    tail = dot(m2l[:, 39 * 384:CLASSES * R], first[0:192, :]).astype(BF16)
    for j in range(4):
        cube[312 + j] = tail[:, 128 * j:128 * j + 128]

    for buffer in (even, odd):
        buffer[...] = jnp.zeros((512, BOX), BF16)

    pair.wait()
    cbuf[chip] = share[...] + share_in[...]

    def far_copies(stage, peers, start, count):
        return [
            pltpu.make_async_remote_copy(
                src_ref=cbuf.at[pl.ds(start, count)],
                dst_ref=cbuf.at[pl.ds(start, count)],
                send_sem=far_send.at[stage, m],
                recv_sem=far_recv.at[stage, m],
                device_id=(peer,),
                device_id_type=MESH,
            )
            for m, peer in enumerate(peers)
        ]

    along_z = far_copies(0, z_peers, chip, 1)
    along_y = far_copies(1, y_peers, (chip // 4) * 4, 4)
    along_x = far_copies(2, x_peers, (chip // 16) * 16, 16)
    for copy in along_z:
        copy.start()

    for distance in DISTANCES:
        @pl.when(valid(distance))
        def _():
            rim_copy(-distance).wait_recv()

        i = slot_of(distance)
        g, side = i // 2, i % 2
        columns = jnp.where(lane < 2 * RIM, rims[i].astype(F32), strips[i].astype(F32))
        wide[i] = columns
        table[R * g:R * g + R, 128 * side:128 * side + 128] = columns.astype(BF16)

    index = iota((256, 128), 0).astype(F32).astype(BF16)

    def one_hot(lo, k):
        pieces = []
        for j in range(3):
            wanted = jnp.broadcast_to(lo[k:k + 1, 128 * j:128 * j + 128], (256, 128))
            pieces.append(
                jnp.where(wanted.astype(BF16) == index, jnp.ones((), BF16), jnp.zeros((), BF16))
            )
        return jnp.concatenate(pieces, axis=1)

    def keep(into, p, value):
        for to, start, count in PLACES[p % 5]:
            at = 256 * (p // 5) + to
            into[at:at + count, :] = value[start:start + count]

    def by_lanes(into, p, sought, v):
        wanted = jnp.broadcast_to(sought[:, 128 * v:128 * v + 128], (R, 128))
        inside, tile = wanted & 127, wanted >> 7
        value = None
        for i in range(BLOCKS):
            moved = jnp.take_along_axis(wide[i], inside, axis=1, mode="promise_in_bounds")
            value = moved if i == 0 else jnp.where(tile == i, moved, value)
        value = value.astype(BF16)
        for to, start, count in PLACES[p % 5]:
            at = 256 * (p // 5) + to
            into[at:at + count, 128 * v:128 * v + 128] = value[start:start + count]

    def by_product(step, into, pair_of):
        lo = [lo_ref[pl.ds(step * 10 + p, 1), :] for p in pair_of]
        hi = [hi_ref[pl.ds(step * 10 + p, 1), :] for p in pair_of]
        hot = jnp.concatenate([one_hot(x, 0) for x in lo], axis=1)
        found = dot(table[...], hot)
        for q, p in enumerate(pair_of):
            wanted = jnp.broadcast_to(hi[q], (R, BOX))
            value = found[0:R, BOX * q:BOX * q + BOX]
            for g in range(1, GROUPS):
                part_of = found[R * g:R * g + R, BOX * q:BOX * q + BOX]
                value = jnp.where(wanted == g, part_of, value)
            keep(into, p, value.astype(BF16))

    def gather(step, into, other):
        sought = {p: cols_ref[pl.ds(step * 10 + p, 1), :] for p in LANE_SLOTS}
        by_product(step, into, PRODUCT_SLOTS[0])
        by_lanes(into, LANE_SLOTS[0], sought[LANE_SLOTS[0]], 0)
        by_lanes(into, LANE_SLOTS[0], sought[LANE_SLOTS[0]], 1)
        by_product(step, into, PRODUCT_SLOTS[1])
        by_lanes(into, LANE_SLOTS[0], sought[LANE_SLOTS[0]], 2)
        translate(step, other, False)
        by_lanes(into, LANE_SLOTS[1], sought[LANE_SLOTS[1]], 0)
        by_product(step, into, PRODUCT_SLOTS[2])
        by_lanes(into, LANE_SLOTS[1], sought[LANE_SLOTS[1]], 1)
        by_lanes(into, LANE_SLOTS[1], sought[LANE_SLOTS[1]], 2)
        by_product(step, into, PRODUCT_SLOTS[3])

    loads[5].wait()
    acc_a[...] = jnp.zeros(acc_a.shape, F32)
    acc_b[...] = jnp.zeros(acc_b.shape, F32)
    at_lane = iota((R, 128), 1).astype(F32).astype(BF16)
    below_48 = at_lane < jnp.full((), 48, BF16)
    below_96 = at_lane < jnp.full((), 96, BF16)

    def translate(step, source, last):
        first_slot = 10 * jnp.maximum(step - 1, 0)
        lhs = []
        for o in range(8):
            tiles = []
            for chunk in range(2):
                ops = []
                for q in range(5):
                    k = first_slot + 5 * chunk + q
                    if last and chunk and q == 4:
                        ops.append(jnp.zeros((R, 128), BF16))
                    else:
                        ops.append(cube[cls[k, o]])
                tiles.append(jnp.where(below_48, ops[0], jnp.where(below_96, ops[1], ops[2])))
                rest = pltpu.roll(ops[2], 32, 1)
                tiles.append(jnp.where(below_48, ops[3], jnp.where(below_96, ops[4], rest)))
            lhs.append(jnp.concatenate(tiles, axis=1))
        acc_a[...] += dot(jnp.concatenate(lhs[0:5], axis=0), source[:, 0:256])
        acc_b[...] += dot(jnp.concatenate(lhs[5:8], axis=0), source[:, 128:384])

    def several(step, _):
        @pl.when(step == 1)
        def _():
            for distance in DISTANCES:
                @pl.when(valid(distance))
                def _():
                    rim_copy(distance).wait_send()
            for copy in along_z:
                copy.wait()
            for copy in along_y:
                copy.start()

        @pl.when(step == 2)
        def _():
            for copy in along_y:
                copy.wait()
            for copy in along_x:
                copy.start()

        gather(6 * step + 0, even, odd)
        gather(6 * step + 1, odd, even)
        gather(6 * step + 2, even, odd)
        gather(6 * step + 3, odd, even)
        gather(6 * step + 4, even, odd)
        gather(6 * step + 5, odd, even)
        return 0

    lax.fori_loop(0, 3, several, 0)
    for copy in along_x:
        copy.wait()

    for load in loads[6:9]:
        load.wait()
    coarse = cbuf[...].reshape(COARSE, 128)
    mixed_far = dot(coup[...], coarse, HIGHEST)
    mine = jnp.sum(
        jnp.where(iota((COARSE, 128), 0) == chip, mixed_far, 0.0), axis=0, keepdims=True
    )
    far = dot_t(jnp.broadcast_to(mine[:, 0:R], (8, R)), cops[...], HIGHEST)
    tile = (iota((R, BOX), 1) % R == iota((R, BOX), 0)).astype(F32)
    far_tiled = dot(far, tile, HIGHEST)
    terms = l2l[...] * far_tiled[0:1, :]
    by_octant = (iota((BOX, BOX), 0) // R == iota((BOX, BOX), 1) // PARENTS).astype(F32)
    lifted = dot(terms, by_octant, HIGHEST)

    gather(STEPS - 1, even, odd)
    translate(STEPS, even, True)
    octant = iota((R, BOX), 1) // PARENTS
    none = jnp.zeros((R, 128), F32)
    sums = jnp.concatenate([acc_a[0:R, :], none], axis=1)
    for o in range(1, 8):
        if o < 5:
            rows = jnp.concatenate([acc_a[R * o:R * o + R, :], none], axis=1)
        else:
            rows = jnp.concatenate([none, acc_b[R * (o - 5):R * (o - 5) + R, :]], axis=1)
        sums = jnp.where(octant == o, rows, sums)
    sums = sums + lifted
    box = iota((R, BOX), 1)
    out_ref[...] = lanes_from(sums, PARENTS * (box % 8) + box // 8)


def shards(multipoles, partners, partner_offset, classes, m2l_ops, m2m_ops, coarse_ops, coupling, l2l_ops):
    any_space = pl.BlockSpec(memory_space=pl.ANY)
    vmem = pl.BlockSpec(memory_space=pltpu.VMEM)
    dma = pltpu.SemaphoreType.DMA
    return pl.pallas_call(
        kernel,
        name="far_field",
        out_shape=(
            jax.ShapeDtypeStruct((R, BOX), F32),
            jax.ShapeDtypeStruct((R, PARENTS), F32),
        ),
        in_specs=[any_space] * 9,
        out_specs=(vmem, vmem),
        scratch_shapes=[
            pltpu.VMEM((R, BOX), BF16),
            pltpu.VMEM((K, BOX), I32),
            pltpu.VMEM((K, BOX), I32),
            pltpu.SMEM((K, 128), I32),
            pltpu.VMEM((R, CLASSES * R), BF16),
            pltpu.VMEM((R, 8 * R), BF16),
            pltpu.VMEM((R, R), F32),
            pltpu.VMEM((COARSE, COARSE), F32),
            pltpu.VMEM((R, 8 * R), F32),
            pltpu.VMEM((R, 128), BF16),
            pltpu.VMEM((BLOCKS, R, 128), BF16),
            pltpu.VMEM((1, 128), F32),
            pltpu.VMEM((1, 128), F32),
            pltpu.VMEM((COARSE, 1, 128), F32),
            pltpu.VMEM((192, BOX), I32),
            pltpu.VMEM((192, BOX), I32),
            pltpu.VMEM((192, BOX), F32),
            pltpu.VMEM((192, BOX), I32),
            pltpu.VMEM((BLOCKS, R, 128), BF16),
            pltpu.VMEM((GROUPS * R, 256), BF16),
            pltpu.VMEM((BLOCKS, R, 128), F32),
            pltpu.VMEM((CLASSES, R, 128), BF16),
            pltpu.VMEM((512, BOX), BF16),
            pltpu.VMEM((512, BOX), BF16),
            pltpu.VMEM((5 * R, 256), F32),
            pltpu.VMEM((3 * R, 256), F32),
            dma((9,)),
            dma((BLOCKS,)),
            dma((BLOCKS,)),
            dma,
            dma,
            dma((3, 3)),
            dma((3, 3)),
        ],
        compiler_params=pltpu.CompilerParams(
            collective_id=0, has_side_effects=True, vmem_limit_bytes=40 * 1024 * 1024
        ),
    )(*[
        pltpu.with_memory_space_constraint(x, pltpu.HBM)
        for x in (
            multipoles, partners, partner_offset, classes, m2l_ops, m2m_ops, coarse_ops, coupling,
            l2l_ops,
        )
    ])


def solution(mesh):
    placed = (
        P(None, "box"), P(None, "box"), P(None, "box"), P(None, "box"),
        P(), P(), P(), P(), P(),
    )
    return jax.shard_map(
        shards,
        mesh=mesh,
        in_specs=placed,
        out_specs=(P(None, "box"), P(None, "box")),
        check_vma=False,
    )
```
